32 devices in a mesh: ctx: 8 (over z, x), head: 4 (over y, core).
Axes of the slice: x: 2, y: 2, z: 4, core: 2. Of those that a mesh axis runs over, the one named last changes fastest.
Arguments:
- queries: bfloat16 [2048, 4096], P('ctx', 'head'), may hold values from -64 to 64
- key_vectors: bfloat16 [2048, 1024], P('ctx', 'head'), may hold values from -4.5 to 4.5
- value_vectors: bfloat16 [2048, 1024], P('ctx', 'head'), may hold values from -6 to 6
- out_weight: bfloat16 [4096, 4096], P('head'), may hold values from -0.09375 to 0.09375
- offsets: int32 [5], replicated, may hold values from 0 to 2048, as said below
Outputs:
- projected: bfloat16 [4096, 2048], P('head', 'ctx')
The draws below stay inside these ranges and needn't reach their ends.
Inputs may be any that keep to these rules, and one draw needn't show every extreme that they name: offsets[0] = 0 and offsets[4] = 2048; offsets rise strictly; every document has 1 to 1024 tokens and one has exactly 1024.
All inputs are finite; a program needn't handle non-finite values.
Results may differ from the reference program's by a relative error of at most 0.014.
Values may be sent and summed in bfloat16 or wider, within the bound.
No kernel may reach another device: no remote copies, remote signals or barrier semaphores. Data moves between devices by JAX's collectives and lax.ppermute only.
A program may use at most 64 MiB of HBM per device.

```python
import jax
import jax.numpy as jnp
from jax import lax

D = 4096
HEADS = 32
KV_HEADS = 8
HEAD_DIM = 128
TOK_DEV = 256
TOKENS = 2048
MAXDOC = 1024
NDOCS = 4
N_HEAD = 4


def drawn_keys(key):
    kv_columns = KV_HEADS * HEAD_DIM
    return jnp.clip(jax.random.normal(key, (TOKENS, kv_columns), jnp.float32), -4.5, 4.5)


def drawn_pair(key):
    key_seed = jax.random.fold_in(key, 11)
    keys_drawn = drawn_keys(key_seed)
    return keys_drawn


def draw_queries(key, part):
    query_columns = HEADS * HEAD_DIM
    query_seed = jax.random.fold_in(key, 21)
    query_draw = jnp.clip(2.5 * jax.random.normal(query_seed, (TOKENS, query_columns), jnp.float32), -12.0, 12.0)
    return query_draw.astype(jnp.bfloat16)


def draw_key_vectors(key, part):
    keys_drawn = drawn_pair(key)
    return keys_drawn.astype(jnp.bfloat16)


def draw_offsets(key, part):
    others = NDOCS - 1
    remaining = TOKENS - MAXDOC
    base_length = remaining // others
    leftover = remaining - base_length * others
    positions = jnp.arange(others, dtype=jnp.int32)
    lengths = base_length + (positions < leftover).astype(jnp.int32)
    pair_count = others // 2
    nudges = jax.random.randint(jax.random.fold_in(key, 31), (pair_count,), -(base_length - 1), base_length).astype(jnp.int32)
    nudge_signed = jnp.zeros((others,), jnp.int32)
    nudge_signed = nudge_signed.at[0:2 * pair_count:2].set(nudges)
    nudge_signed = nudge_signed.at[1:2 * pair_count:2].set(-nudges)
    lengths = lengths + nudge_signed
    long_index = jax.random.randint(jax.random.fold_in(key, 32), (), 0, NDOCS).astype(jnp.int32)
    slots = jnp.arange(NDOCS, dtype=jnp.int32)
    before = lengths[jnp.minimum(slots, others - 1)]
    after = lengths[jnp.maximum(slots - 1, 0)]
    all_lengths = jnp.where(slots < long_index, before, jnp.where(slots == long_index, MAXDOC, after)).astype(jnp.int32)
    return jnp.concatenate([jnp.zeros((1,), jnp.int32), jnp.cumsum(all_lengths).astype(jnp.int32)])


def steps_of(key, shape, split, low, largest):
    level = 1.0
    for axis_at, blocks in split:
        draws = jax.random.uniform(jax.random.fold_in(jax.random.fold_in(key, 6), axis_at), (blocks,), jnp.float32, low / len(split), largest / len(split))
        level = level * jnp.repeat(jnp.exp(draws), shape[axis_at] // blocks).reshape((-1,) + (1,) * (len(shape) - 1 - axis_at))
    return level


def normal_values(rng, extent, deviation, limit, cuts=(), kind=jnp.bfloat16):
    array = jax.random.normal(rng, extent, jnp.float32) * deviation
    if len(cuts) > 0:
        array = steps_of(rng, extent, cuts, -0.22, 0.18) * array
    return jnp.clip(array, min=-limit, max=limit).astype(kind)


def setup_inputs(seed: int = 0) -> dict:
    streams_of = jax.random.split(jax.random.key(seed), 6)
    return {
        "queries": draw_queries(jax.random.fold_in(streams_of[5], 71), 0),
        "key_vectors": draw_key_vectors(jax.random.fold_in(streams_of[5], 71), 0),
        "value_vectors": normal_values(streams_of[2], (TOKENS, KV_HEADS * HEAD_DIM), 1.0, 6.0, ((0, 8), (1, 4))),
        "out_weight": normal_values(streams_of[3], (HEADS * HEAD_DIM, D), (HEADS * HEAD_DIM) ** -0.5, 0.09375, ((0, 4),)),
        "offsets": draw_offsets(jax.random.fold_in(streams_of[5], 71), 0),
    }


def doc_index(positions, offsets):
    boundaries = offsets[1:-1]
    return jnp.sum((positions[:, None] >= boundaries[None, :]).astype(jnp.int32), axis=1)


def reference(queries, key_vectors, value_vectors, out_weight, offsets):
    group_size = HEADS // KV_HEADS
    logit_scale = HEAD_DIM ** -0.5
    window = MAXDOC
    padding = jnp.zeros((window, KV_HEADS * HEAD_DIM), key_vectors.dtype)
    padded_keys = jnp.concatenate([padding, key_vectors], axis=0)
    padded_values = jnp.concatenate([padding, value_vectors], axis=0)

    def attend_block(block_index):
        row_start = (block_index * TOK_DEV).astype(jnp.int32)
        query_tile_rows = lax.dynamic_slice_in_dim(queries, row_start, TOK_DEV, 0).astype(jnp.float32)
        query_tile_rows = query_tile_rows.reshape(TOK_DEV, KV_HEADS, group_size, HEAD_DIM)
        key_tile_rows = lax.dynamic_slice_in_dim(padded_keys, row_start, window + TOK_DEV, 0).astype(jnp.float32)
        key_tile_rows = key_tile_rows.reshape(window + TOK_DEV, KV_HEADS, HEAD_DIM)
        value_tile_rows = lax.dynamic_slice_in_dim(padded_values, row_start, window + TOK_DEV, 0).astype(jnp.float32)
        value_tile_rows = value_tile_rows.reshape(window + TOK_DEV, KV_HEADS, HEAD_DIM)
        query_pos = row_start + jnp.arange(TOK_DEV, dtype=jnp.int32)
        key_pos = row_start - window + jnp.arange(window + TOK_DEV, dtype=jnp.int32)
        query_doc = doc_index(query_pos, offsets)
        key_doc = doc_index(key_pos, offsets)
        visible = (key_pos[None, :] >= 0) & (key_pos[None, :] <= query_pos[:, None]) & (key_doc[None, :] == query_doc[:, None])
        attention_logits = jnp.einsum("myqe,cye->yqmc", query_tile_rows, key_tile_rows) * logit_scale
        attention_logits = jnp.where(visible, attention_logits, -jnp.inf)
        row_max = jnp.max(attention_logits, axis=-1, keepdims=True)
        exponent = jnp.exp(attention_logits - row_max)
        row_sum = jnp.sum(exponent, axis=-1)
        attention_probs = lax.optimization_barrier(exponent.astype(jnp.bfloat16)).astype(jnp.float32)
        weighted_values = jnp.einsum("avmk,kab->mavb", attention_probs, value_tile_rows)
        attended = weighted_values / jnp.transpose(row_sum, (2, 0, 1))[..., None]
        return attended.reshape(TOK_DEV, HEADS * HEAD_DIM).astype(jnp.bfloat16)

    attended = lax.map(attend_block, jnp.arange(TOKENS // TOK_DEV, dtype=jnp.int32))
    attended = attended.reshape(TOKENS, HEADS * HEAD_DIM)
    group_cols = HEADS * HEAD_DIM // N_HEAD

    def add_group(group_index, accumulated):
        first_col = (group_index * group_cols).astype(jnp.int32)
        attended_cols = lax.dynamic_slice_in_dim(attended, first_col, group_cols, 1)
        weight_rows = lax.dynamic_slice_in_dim(out_weight, first_col, group_cols, 0)
        partial_value = jnp.dot(attended_cols, weight_rows, preferred_element_type=jnp.float32).astype(jnp.bfloat16)
        partial_value = lax.optimization_barrier(partial_value)
        return accumulated + partial_value.astype(jnp.float32)

    summed = lax.fori_loop(0, N_HEAD, add_group, jnp.zeros((TOKENS, D), jnp.float32))
    return jnp.transpose(summed).astype(jnp.bfloat16)
```

```python
import jax
import jax.numpy as jnp
from jax import lax
from jax.experimental import pallas as pl
from jax.experimental.pallas import tpu as pltpu
from jax.sharding import PartitionSpec as P

HEAD_DIM = 128
REACH = 15
LOG2E = 1.4426950408889634
masked_score = -1e30
VMEM_LIMIT = 48 * 1024 * 1024

vmem = pl.BlockSpec(memory_space=pltpu.VMEM)
smem = pl.BlockSpec(memory_space=pltpu.SMEM)
anywhere = pl.BlockSpec(memory_space=pl.ANY)


def params():
    return pltpu.CompilerParams(vmem_limit_bytes=VMEM_LIMIT)


def document_starts(where, rows):
    first = where[0] * rows
    positions = first + lax.broadcasted_iota(jnp.int32, (1, rows), 1)
    starts = jnp.zeros((1, rows), jnp.int32)
    start_first = jnp.int32(0)
    start_last = jnp.int32(0)
    for i in range(2, where.shape[0] - 1):
        edge = where[i]
        starts = jnp.where(positions >= edge, edge, starts)
        start_first = jnp.where(first >= edge, edge, start_first)
        start_last = jnp.where(first + rows - 1 >= edge, edge, start_last)
    return positions, starts, start_first, start_last


def scores_of(keys, query):
    return lax.dot_general(keys, query, (((1,), (1,)), ((), ())), preferred_element_type=jnp.float32)


def attend_piece(q_ref, kv_ref, group, heads, before, after, key_start, positions, starts):
    rows = kv_ref.shape[0]
    factor = HEAD_DIM ** -0.5 * LOG2E
    keys = kv_ref[:, :HEAD_DIM]
    values = kv_ref[:, HEAD_DIM:].T
    key_pos = key_start + lax.broadcasted_iota(jnp.int32, (rows, 1), 0)
    visible = key_pos >= starts
    if before is None:
        visible = visible & (key_pos <= positions)
    for i in range(heads):
        h = group * heads + i
        s = scores_of(keys, q_ref[:, h * HEAD_DIM : (h + 1) * HEAD_DIM])
        s = jnp.where(visible, s, masked_score)
        top = jnp.max(s, axis=0, keepdims=True)
        if before is not None:
            old_top = before[0][i : i + 1, :]
            top = jnp.maximum(old_top, top)
        p = jnp.exp2((s - top) * factor)
        total = jnp.sum(p, axis=0, keepdims=True)
        out = jnp.dot(values, p.astype(jnp.bfloat16), preferred_element_type=jnp.float32)
        if before is not None:
            alpha = jnp.exp2((old_top - top) * factor)
            total = before[1][i : i + 1, :] * alpha + total
            out = before[2][i] * alpha + out
        after[0][i : i + 1, :] = top
        after[1][i : i + 1, :] = total
        after[2][i] = out


def attend_pieces(where, q_ref, pieces, before, after, heads):
    rows = q_ref.shape[0]
    me = where[0]
    positions, starts, start_first, _ = document_starts(where, rows)
    current = dict(before)
    for kv_ref, group, back, own in pieces:
        key_start = (me - back(lax.rem(me, 2))) * rows
        if own:
            attend_piece(q_ref, kv_ref, group, heads, None, after[group], key_start, positions, starts)
        else:
            seen = (key_start >= 0) & (key_start + rows > start_first)
            source = current[group]

            @pl.when(seen)
            def _():
                attend_piece(q_ref, kv_ref, group, heads, source, after[group], key_start, positions, starts)

            if source is not after[group]:

                @pl.when(jnp.logical_not(seen))
                def _():
                    for old, new in zip(source, after[group]):
                        new[...] = old[...]

        current[group] = after[group]


def state_shapes(heads, rows):
    return [(heads, rows), (heads, rows), (heads, HEAD_DIM, rows)]


def by_threes(refs, groups):
    return {g: refs[3 * i : 3 * i + 3] for i, g in enumerate(groups)}


def attend_call(where, q, pieces, state, n_groups):
    rows, width = q.shape
    heads = width // HEAD_DIM // n_groups
    touched = sorted({p[1] for p in pieces})
    given = [a for g in touched for a in state.get(g, ())]

    def kernel(where_ref, q_ref, *refs):
        kvs = refs[: len(pieces)]
        before = by_threes(refs[len(pieces) : len(pieces) + len(given)], touched) if given else {}
        after = by_threes(refs[len(pieces) + len(given) :], touched)
        attend_pieces(where_ref, q_ref, [(r, *p[1:]) for r, p in zip(kvs, pieces)], before, after, heads)

    shapes = [jax.ShapeDtypeStruct(s, jnp.float32) for s in state_shapes(heads, rows) * len(touched)]
    first = 2 + len(pieces)
    outs = pl.pallas_call(
        kernel,
        out_shape=shapes,
        in_specs=[smem] + [vmem] * (1 + len(pieces) + len(given)),
        out_specs=[vmem] * len(shapes),
        input_output_aliases={first + i: i for i in range(len(given))},
        compiler_params=params(),
        name="attend",
    )(where, q, *[p[0] for p in pieces], *given)
    return {**state, **by_threes(outs, touched)}


def finish_call(where, q, pieces, state, n_groups):
    rows, width = q.shape
    n_heads = width // HEAD_DIM
    heads = n_heads // n_groups
    groups = range(n_groups)
    given = [a for g in groups for a in state[g]]

    def kernel(where_ref, q_ref, *refs):
        kvs = refs[: len(pieces)]
        before = by_threes(refs[len(pieces) : len(pieces) + len(given)], groups)
        out_ref = refs[len(pieces) + len(given)]
        after = by_threes(refs[len(pieces) + len(given) + 1 :], groups)
        attend_pieces(where_ref, q_ref, [(r, *p[1:]) for r, p in zip(kvs, pieces)], before, after, heads)
        for h in range(n_heads):
            _, total_ref, acc_ref = after[h // heads]
            i = h % heads
            head = acc_ref[i] / total_ref[i : i + 1, :]
            out_ref[:, h * HEAD_DIM : (h + 1) * HEAD_DIM] = head.T.astype(jnp.bfloat16)

    return pl.pallas_call(
        kernel,
        out_shape=jax.ShapeDtypeStruct((rows, width), jnp.bfloat16),
        in_specs=[smem] + [vmem] * (1 + len(pieces) + len(given)),
        out_specs=vmem,
        scratch_shapes=[pltpu.VMEM(s, jnp.float32) for s in state_shapes(heads, rows) * n_groups],
        compiler_params=params(),
        name="finish",
    )(where, q, *[p[0] for p in pieces], *given)


def project_call(attended, out_weight, blocks, block, added, out_type, name):
    rows, depth = attended.shape
    count = len(blocks)

    def kernel(order_ref, att_ref, w_ref, *refs):
        out_ref, w_scratch, sems = refs[-3:]
        copies = []
        for i in range(count):
            start = pl.multiple_of(order_ref[i] * block, block)
            copy = pltpu.make_async_copy(w_ref.at[:, pl.ds(start, block)], w_scratch.at[i], sems.at[i])
            copy.start()
            copies.append(copy)
        for i in range(count):
            copies[i].wait()
            value = jnp.dot(att_ref[...], w_scratch[i], preferred_element_type=jnp.float32)
            if added is not None:
                value = value + refs[0][i].astype(jnp.float32)
            out_ref[i] = value.astype(out_type)

    more = [] if added is None else [added]
    return pl.pallas_call(
        kernel,
        out_shape=jax.ShapeDtypeStruct((count, rows, block), out_type),
        in_specs=[smem, vmem, anywhere] + [vmem] * len(more),
        out_specs=vmem,
        scratch_shapes=[pltpu.VMEM((count, depth, block), jnp.bfloat16), pltpu.SemaphoreType.DMA((count,))],
        compiler_params=params(),
        name=name,
    )(jnp.stack(blocks).astype(jnp.int32), attended, out_weight, *more)


def output_call(kept, arrived):
    rows, block = kept.shape

    def kernel(kept_ref, arrived_ref, out_ref):
        out_ref[...] = (kept_ref[...] + arrived_ref[...].astype(jnp.float32)).T.astype(jnp.bfloat16)

    return pl.pallas_call(
        kernel,
        out_shape=jax.ShapeDtypeStruct((block, rows), jnp.bfloat16),
        in_specs=[vmem] * 2,
        out_specs=vmem,
        compiler_params=params(),
        name="output",
    )(kept, arrived)


def swapped(array, axis, bit):
    return lax.ppermute(array, axis, [(i, i ^ bit) for i in range(lax.axis_size(axis))])


def projected(attended, out_weight):
    count = lax.axis_size("head")
    block = out_weight.shape[1] // count
    me = lax.axis_index("head")
    if count < 4 or count & (count - 1):
        whole = jnp.dot(attended, out_weight, preferred_element_type=jnp.float32).astype(jnp.bfloat16)
        return lax.psum_scatter(whole, "head", scatter_dimension=1, tiled=True).T
    mine = [(me >> b) & 1 for b in range(count.bit_length() - 1)]

    def blocks(bit0, bit1):
        return [bit0 + 2 * bit1 + 4 * i for i in range(count // 4)]

    send_far = project_call(attended, out_weight, blocks(1 - mine[0], 1 - mine[1]), block, None, jnp.bfloat16, "p0")
    got_far = swapped(send_far, "head", 1)
    send_near = project_call(attended, out_weight, blocks(1 - mine[0], mine[1]), block, None, jnp.bfloat16, "p1")
    got_near = swapped(send_near, "head", 1)
    far = project_call(attended, out_weight, blocks(mine[0], 1 - mine[1]), block, got_far, jnp.bfloat16, "p2")
    got = swapped(far, "head", 2)
    kept = project_call(attended, out_weight, blocks(mine[0], mine[1]), block, got_near, jnp.float32, "p3")
    for b in range(2, len(mine)):
        kept = kept + got.astype(jnp.float32)
        pairs = kept.reshape(kept.shape[0] // 2, 2, *kept.shape[1:])
        sent = lax.dynamic_index_in_dim(pairs, 1 - mine[b], 1, keepdims=False)
        kept = lax.dynamic_index_in_dim(pairs, mine[b], 1, keepdims=False)
        got = swapped(sent.astype(jnp.bfloat16), "head", 1 << b)
    return output_call(kept[0], got[0])


def on_device(queries, key_vectors, value_vectors, out_weight, offsets):
    rows = queries.shape[0]
    groups = key_vectors.shape[1] // HEAD_DIM
    devices = lax.axis_size("ctx")
    me = lax.axis_index("ctx")
    odd = lax.rem(me, 2) == 1
    pair_steps = (min(REACH, devices // 2) + 1) // 2
    where = jnp.concatenate([me[None].astype(jnp.int32), offsets])

    def shifted(block):
        return lax.ppermute(block, "ctx", [(i, (i + 2) % devices) for i in range(devices)])

    def piece(g):
        cut = slice(g * HEAD_DIM, (g + 1) * HEAD_DIM)
        return jnp.concatenate([key_vectors[:, cut], value_vectors[:, cut]], axis=1)

    own = [piece(g) for g in range(groups)]
    moving = own
    state = attend_call(where, queries, [(own[g], g, lambda x: 0, True) for g in range(groups)], {}, groups)
    for step in range(1, pair_steps + 1):
        moving = [shifted(m) for m in moving]
        last = step == pair_steps
        across = [swapped(jnp.where(odd, m, o) if last else m, "ctx", 1) for m, o in zip(moving, own)]
        back = (lambda x, step=step: jnp.where(x == 1, 1, 2 * step - 1)) if last else (lambda x, step=step: 2 * step - 1 + 2 * x)
        pieces = [(moving[g], g, lambda x, step=step: 2 * step, False) for g in range(groups)]
        state = attend_call(where, queries, pieces, state, groups)
        pieces = [(across[g], g, back, False) for g in range(groups)]
        if last:
            attended = finish_call(where, queries, pieces, state, groups)
        else:
            state = attend_call(where, queries, pieces, state, groups)
    return projected(attended, out_weight)


def solution(mesh):
    placed = (P("ctx", "head"), P("ctx", "head"), P("ctx", "head"), P("head", None), P())
    return jax.shard_map(
        on_device, mesh=mesh, in_specs=placed, out_specs=P("head", "ctx"), check_vma=False
    )
```

```python
import jax
import jax.numpy as jnp
from jax import lax
from jax.experimental import pallas as pl
from jax.experimental.pallas import tpu as pltpu
from jax.sharding import PartitionSpec as P

HEAD_DIM = 128
REACH = 15
LOG2E = 1.4426950408889634
masked_score = -1e30
WEIGHT_COPIES = 8
VMEM_LIMIT = 20 * 1024 * 1024

vmem = pl.BlockSpec(memory_space=pltpu.VMEM)
smem = pl.BlockSpec(memory_space=pltpu.SMEM)
hbm = pl.BlockSpec(memory_space=pltpu.HBM)


def in_hbm(array):
    return pltpu.with_memory_space_constraint(array, pltpu.HBM)


def in_vmem(arrays):
    return [pltpu.with_memory_space_constraint(a, pltpu.VMEM) for a in arrays]


def params():
    return pltpu.CompilerParams(vmem_limit_bytes=VMEM_LIMIT)


def document_starts(offsets, first, rows):
    positions = first + lax.broadcasted_iota(jnp.int32, (1, rows), 1)
    starts = jnp.zeros((1, rows), jnp.int32)
    for i in range(1, offsets.shape[0] - 1):
        starts = jnp.where(positions >= offsets[i], offsets[i], starts)
    return starts


def scores_of(keys, query):
    return lax.dot_general(keys, query, (((1,), (1,)), ((), ())), preferred_element_type=jnp.float32)


def visible_keys(starts, key_start, rows, first):
    key_pos = key_start + lax.broadcasted_iota(jnp.int32, (rows, 1), 0)
    visible = key_pos >= starts
    if first is not None:
        visible = visible & (key_pos <= first + lax.broadcasted_iota(jnp.int32, (1, rows), 1))
    return visible


def score_block(q_ref, k_ref, visible, before):
    factor = HEAD_DIM ** -0.5 * LOG2E
    heads = q_ref.shape[1] // HEAD_DIM
    each = heads // (k_ref.shape[1] // HEAD_DIM)
    groups = [h // each for h in range(heads)]
    scores = [
        scores_of(k_ref[:, g * HEAD_DIM : (g + 1) * HEAD_DIM], q_ref[:, h * HEAD_DIM : (h + 1) * HEAD_DIM])
        for h, g in enumerate(groups)
    ]
    scores = [jnp.where(visible, s, masked_score) for s in scores]
    tops = [jnp.max(s, axis=0, keepdims=True) for s in scores]
    if before is not None:
        olds = [before[0][h : h + 1, :] for h in range(heads)]
        tops = [jnp.maximum(old, top) for old, top in zip(olds, tops)]
    weights = [jnp.exp2((s - top) * factor) for s, top in zip(scores, tops)]
    totals = [jnp.sum(w, axis=0, keepdims=True) for w in weights]
    weights = [w.astype(jnp.bfloat16) for w in weights]
    if before is None:
        return tops, totals, weights, None
    alphas = [jnp.exp2((old - top) * factor) for old, top in zip(olds, tops)]
    totals = [before[1][h : h + 1, :] * alphas[h] + totals[h] for h in range(heads)]
    return tops, totals, weights, alphas


def value_block(v_ref, weights, alphas, acc_ref):
    groups = v_ref.shape[1] // HEAD_DIM
    each = len(weights) // groups
    values = [v_ref[:, g * HEAD_DIM : (g + 1) * HEAD_DIM].T for g in range(groups)]
    sums = [jnp.dot(values[h // each], w, preferred_element_type=jnp.float32) for h, w in enumerate(weights)]
    if alphas is None:
        return sums
    return [acc_ref[h] * alphas[h] + s for h, s in enumerate(sums)]


def store_rows(ref, rows):
    for h, row in enumerate(rows):
        ref[h : h + 1, :] = row


def state_shapes(heads, rows):
    return [
        jax.ShapeDtypeStruct((heads, rows), jnp.float32),
        jax.ShapeDtypeStruct((heads, rows), jnp.float32),
        jax.ShapeDtypeStruct((heads, HEAD_DIM, rows), jnp.float32),
    ]


def first_row(rows):
    return lax.axis_index("ctx") * rows


def weight_shape(out_weight, count):
    return jax.ShapeDtypeStruct((out_weight.shape[0], out_weight.shape[1] // 4), out_weight.dtype)


def weight_copies(w_ref, parts, sems, far_core, far_next, count):
    depth = w_ref.shape[0]
    block = w_ref.shape[1] // count
    me = lax.axis_index("head")
    bits = (me % 2 + far_core) % 2 + 2 * ((me // 2 + far_next) % 2)
    pieces = sems.shape[0] // (count // 4)
    step = depth // pieces
    copies = []
    for i in range(count // 4):
        columns = pl.ds(pl.multiple_of((bits + 4 * i) * block, block), block)
        for j in range(pieces):
            rows = slice(j * step, (j + 1) * step)
            source = w_ref.at[rows, columns]
            target = parts.at[rows, i * block : (i + 1) * block]
            copies.append(pltpu.make_async_copy(source, target, sems.at[i * pieces + j]))
    return copies


def own_call(offsets, q, keys, values, out_weight, count):
    rows, width = q.shape

    def kernel(offsets_ref, q_in, k_in, v_in, w_in, starts_ref, q_ref, k_ref, v_ref, w_ref, top_ref, total_ref, acc_ref, sems, w_sems):
        copies = [
            pltpu.make_async_copy(source, target, sems.at[i])
            for i, (source, target) in enumerate(((k_in, k_ref), (q_in, q_ref), (v_in, v_ref)))
        ]
        weight = weight_copies(w_in, w_ref, w_sems, 1, 1, count)
        for copy in copies + weight:
            copy.start()
        first = first_row(rows)
        starts = document_starts(offsets_ref, first, rows)
        starts_ref[...] = starts
        visible = visible_keys(starts, first, rows, first)
        for copy in copies:
            copy.wait()
        tops, totals, weights, _ = score_block(q_ref, k_ref, visible, None)
        store_rows(top_ref, tops)
        store_rows(total_ref, totals)
        for h, out in enumerate(value_block(v_ref, weights, None, None)):
            acc_ref[h] = out
        for copy in weight:
            copy.wait()

    outs = pl.pallas_call(
        kernel,
        out_shape=[
            jax.ShapeDtypeStruct((1, rows), jnp.int32),
            *[jax.ShapeDtypeStruct(x.shape, x.dtype) for x in (q, keys, values)],
            weight_shape(out_weight, count),
            *state_shapes(width // HEAD_DIM, rows),
        ],
        in_specs=[smem] + [hbm] * 4,
        out_specs=[vmem] * 8,
        scratch_shapes=[pltpu.SemaphoreType.DMA((3,)), pltpu.SemaphoreType.DMA((count // 4 * WEIGHT_COPIES,))],
        compiler_params=params(),
        cost_estimate=cost(width, rows, 1),
        name="own",
    )(offsets, *[in_hbm(x) for x in (q, keys, values, out_weight)])
    return outs[:5], outs[5:]


def cost(width, rows, blocks):
    return pl.CostEstimate(flops=4 * width * rows * rows * blocks, bytes_accessed=0, transcendentals=width // HEAD_DIM * rows * rows * blocks)


def attend_call(starts, q, pieces, state, out_weight, kinds, count):
    rows, width = q.shape
    n = len(pieces)

    def kernel(starts_ref, q_ref, *refs):
        before, w_in = refs[2 * n : 2 * n + 3], refs[2 * n + 3]
        after, parts = refs[2 * n + 4 : 2 * n + 7], refs[2 * n + 7 : 2 * n + 7 + len(kinds)]
        sems = refs[-1]
        copies = []
        for i, (part, kind) in enumerate(zip(parts, kinds)):
            copies += weight_copies(w_in, part, sems.at[i], *kind, count)
        for copy in copies:
            copy.start()
        for i, (_, _, back) in enumerate(pieces):
            k_ref, v_ref = refs[2 * i : 2 * i + 2]
            position = lax.axis_index("ctx")
            key_start = (position - back(lax.rem(position, 2))) * rows
            visible = visible_keys(starts_ref[...], key_start, rows, None)
            source = before if i == 0 else after
            tops, totals, weights, alphas = score_block(q_ref, k_ref, visible, source)
            store_rows(after[0], tops)
            store_rows(after[1], totals)
            for h, out in enumerate(value_block(v_ref, weights, alphas, source[2])):
                after[2][h] = out
        for copy in copies:
            copy.wait()

    first = 2 + 2 * n
    outs = pl.pallas_call(
        kernel,
        out_shape=[*state_shapes(width // HEAD_DIM, rows), *[weight_shape(out_weight, count)] * len(kinds)],
        in_specs=[vmem] * (first + 3) + [hbm],
        out_specs=[vmem] * (3 + len(kinds)),
        scratch_shapes=[pltpu.SemaphoreType.DMA((max(len(kinds), 1), count // 4 * WEIGHT_COPIES))],
        input_output_aliases={first + i: i for i in range(3)},
        compiler_params=params(),
        cost_estimate=cost(width, rows, n),
        name="attend",
    )(*in_vmem([starts, q, *[a for p in pieces for a in p[:2]], *state]), in_hbm(out_weight))
    return outs[:3], outs[3:]


def last_scores_call(starts, q, keys, back, state):
    rows, width = q.shape
    heads = width // HEAD_DIM

    def kernel(starts_ref, q_ref, k_ref, top_ref, old_total_ref, total_ref, alpha_ref, weights_ref):
        position = lax.axis_index("ctx")
        key_start = (position - back(lax.rem(position, 2))) * rows
        visible = visible_keys(starts_ref[...], key_start, rows, None)
        _, totals, weights, alphas = score_block(q_ref, k_ref, visible, (top_ref, old_total_ref))
        store_rows(total_ref, totals)
        store_rows(alpha_ref, alphas)
        for h, w in enumerate(weights):
            weights_ref[h] = w

    return pl.pallas_call(
        kernel,
        out_shape=[
            jax.ShapeDtypeStruct((heads, rows), jnp.float32),
            jax.ShapeDtypeStruct((heads, rows), jnp.float32),
            jax.ShapeDtypeStruct((heads, rows, rows), jnp.bfloat16),
        ],
        in_specs=[vmem] * 5,
        out_specs=[vmem] * 3,
        compiler_params=params(),
        cost_estimate=cost(width, rows, 1),
        name="last_scores",
    )(*in_vmem([starts, q, keys, state[0], state[1]]))


def project_into(out_ref, att_ref, w_ref, added_ref):
    block = out_ref.shape[2]
    step = min(block, 256)
    for i in range(out_ref.shape[0]):
        for start in range(0, block, step):
            cut = slice(start, start + step)
            columns = w_ref[:, i * block + start : i * block + start + step]
            value = jnp.dot(att_ref[...], columns, preferred_element_type=jnp.float32)
            if added_ref is not None:
                value = value + added_ref[i, :, cut].astype(jnp.float32)
            out_ref[i, :, cut] = value.astype(out_ref.dtype)


def finish_call(values, weights, totals, alphas, acc, w_far, count):
    heads, _, rows = acc.shape
    block = w_far.shape[1] * 4 // count

    def kernel(v_ref, p_ref, total_ref, alpha_ref, acc_ref, w_ref, att_ref, far_ref):
        scales = [alpha_ref[h : h + 1, :] for h in range(heads)]
        outs = value_block(v_ref, [p_ref[h] for h in range(heads)], scales, acc_ref)
        for h, out in enumerate(outs):
            head = out * (1.0 / total_ref[h : h + 1, :])
            att_ref[:, h * HEAD_DIM : (h + 1) * HEAD_DIM] = head.T.astype(jnp.bfloat16)
        project_into(far_ref, att_ref, w_ref, None)

    return pl.pallas_call(
        kernel,
        out_shape=[
            jax.ShapeDtypeStruct((rows, heads * HEAD_DIM), jnp.bfloat16),
            jax.ShapeDtypeStruct((count // 4, rows, block), jnp.bfloat16),
        ],
        in_specs=[vmem] * 6,
        out_specs=[vmem] * 2,
        compiler_params=params(),
        name="finish",
    )(*in_vmem([values, weights, totals, alphas, acc, w_far]))


def project_call(attended, weight, added, count, out_type, name):
    rows, depth = attended.shape
    block = weight.shape[1] * 4 // count

    def kernel(att_ref, w_ref, *refs):
        project_into(refs[-1], att_ref, w_ref, refs[0] if len(refs) > 1 else None)

    more = [] if added is None else [added]
    return pl.pallas_call(
        kernel,
        out_shape=jax.ShapeDtypeStruct((count // 4, rows, block), out_type),
        in_specs=[vmem] * (2 + len(more)),
        out_specs=vmem,
        compiler_params=params(),
        cost_estimate=pl.CostEstimate(flops=2 * rows * depth * weight.shape[1], bytes_accessed=0, transcendentals=0),
        name=name,
    )(*in_vmem([attended, weight, *more]))


def kept_call(attended, out_weight, added, count):
    rows, depth = attended.shape
    part = weight_shape(out_weight, count)

    def kernel(att_ref, w_in, added_ref, out_ref, w_ref, sems):
        copies = weight_copies(w_in, w_ref, sems, 0, 0, count)
        for copy in copies:
            copy.start()
        for copy in copies:
            copy.wait()
        project_into(out_ref, att_ref, w_ref, added_ref)

    return pl.pallas_call(
        kernel,
        out_shape=jax.ShapeDtypeStruct(added.shape, jnp.float32),
        in_specs=[vmem, hbm, vmem],
        out_specs=vmem,
        scratch_shapes=[pltpu.VMEM(part.shape, part.dtype), pltpu.SemaphoreType.DMA((count // 4 * WEIGHT_COPIES,))],
        compiler_params=params(),
        cost_estimate=pl.CostEstimate(flops=2 * rows * depth * part.shape[1], bytes_accessed=0, transcendentals=0),
        name="kept",
    )(*in_vmem([attended]), in_hbm(out_weight), *in_vmem([added]))


def pick_call(moving, own):
    def kernel(moving_ref, own_ref, out_ref):
        odd = lax.rem(lax.axis_index("ctx"), 2) == 1

        @pl.when(odd)
        def _():
            out_ref[...] = moving_ref[...]

        @pl.when(jnp.logical_not(odd))
        def _():
            out_ref[...] = own_ref[...]

    return pl.pallas_call(
        kernel,
        out_shape=jax.ShapeDtypeStruct(own.shape, own.dtype),
        in_specs=[vmem] * 2,
        out_specs=vmem,
        compiler_params=params(),
        name="pick",
    )(*in_vmem([moving, own]))


def output_call(kept, arrived):
    rows, block = kept.shape

    def kernel(kept_ref, arrived_ref, out_ref):
        out_ref[...] = (kept_ref[...] + arrived_ref[...].astype(jnp.float32)).T.astype(jnp.bfloat16)

    return pl.pallas_call(
        kernel,
        out_shape=jax.ShapeDtypeStruct((block, rows), jnp.bfloat16),
        in_specs=[vmem] * 2,
        out_specs=vmem,
        compiler_params=params(),
        name="output",
    )(kept, arrived)


def swapped(array, axis, bit):
    return lax.ppermute(array, axis, [(i, i ^ bit) for i in range(lax.axis_size(axis))])


def summed_over_heads(attended, far, weights, out_weight, count):
    w_near, w_sent = weights
    got_far = swapped(far, "head", 1)
    near = project_call(attended, w_near, None, count, jnp.bfloat16, "near")
    got_near = swapped(near, "head", 1)
    sent = project_call(attended, w_sent, got_far, count, jnp.bfloat16, "sent")
    got = swapped(sent, "head", 2)
    kept = kept_call(attended, out_weight, got_near, count)
    me = lax.axis_index("head")
    for b in range(2, count.bit_length() - 1):
        kept = kept + got.astype(jnp.float32)
        pairs = kept.reshape(kept.shape[0] // 2, 2, *kept.shape[1:])
        bit = (me >> b) & 1
        sent = lax.dynamic_index_in_dim(pairs, 1 - bit, 1, keepdims=False)
        kept = lax.dynamic_index_in_dim(pairs, bit, 1, keepdims=False)
        got = swapped(sent.astype(jnp.bfloat16), "head", 1 << b)
    return output_call(kept[0], got[0])


def on_device(queries, key_vectors, value_vectors, out_weight, offsets):
    devices = lax.axis_size("ctx")
    heads = lax.axis_size("head")
    pair_steps = (min(REACH, devices // 2) + 1) // 2

    def shifted(block):
        return lax.ppermute(block, "ctx", [(i, (i + 2) % devices) for i in range(devices)])

    moving = (key_vectors, value_vectors)
    (starts, q, keys, values, w_far), state = own_call(offsets, queries, key_vectors, value_vectors, out_weight, heads)
    waiting, brought = [], []
    for step in range(1, pair_steps + 1):
        moving = tuple(shifted(m) for m in moving)
        first, state = lax.optimization_barrier((moving[0], state))
        moving = (first, moving[1])
        waiting.append((*moving, lambda x, step=step: 2 * step))
        if step < pair_steps:
            across = tuple(swapped(m, "ctx", 1) for m in moving)
            kinds = [(1, 0)] if step == 1 else []
            state, more = attend_call(starts, q, waiting, state, out_weight, kinds, heads)
            brought += [*more]
            waiting = [(*across, lambda x, step=step: 2 * step - 1 + 2 * x)]
    across = tuple(swapped(pick_call(m, o), "ctx", 1) for m, o in zip(moving, (keys, values)))
    kinds = [(0, 1)] if brought else [(1, 0), (0, 1)]
    state, more = attend_call(starts, q, waiting, state, out_weight, kinds, heads)

    def back(x):
        return jnp.where(x == 1, 1, 2 * pair_steps - 1)

    totals, alphas, weights = last_scores_call(starts, q, across[0], back, state)
    attended, far = finish_call(across[1], weights, totals, alphas, state[2], w_far, heads)
    return summed_over_heads(attended, far, brought + [*more], out_weight, heads)


def solution(mesh):
    placed = (P("ctx", "head"), P("ctx", "head"), P("ctx", "head"), P("head", None), P())
    return jax.shard_map(
        on_device, mesh=mesh, in_specs=placed, out_specs=P("head", "ctx"), check_vma=False
    )
```

```python
import jax
import jax.numpy as jnp
from jax import lax
from jax.experimental import pallas as pl
from jax.experimental.pallas import tpu as pltpu
from jax.sharding import PartitionSpec as P

HEAD_DIM = 128
REACH = 15
LOG2E = 1.4426950408889634
masked_score = -1e30
PARTS = 2
VMEM_LIMIT = 20 * 1024 * 1024

vmem = pl.BlockSpec(memory_space=pltpu.VMEM)
smem = pl.BlockSpec(memory_space=pltpu.SMEM)
hbm = pl.BlockSpec(memory_space=pltpu.HBM)


def in_hbm(array):
    return pltpu.with_memory_space_constraint(array, pltpu.HBM)


def in_vmem(arrays):
    return [pltpu.with_memory_space_constraint(a, pltpu.VMEM) for a in arrays]


def params():
    return pltpu.CompilerParams(vmem_limit_bytes=VMEM_LIMIT)


def document_starts(offsets, first, rows):
    positions = first + lax.broadcasted_iota(jnp.int32, (1, rows), 1)
    starts = jnp.zeros((1, rows), jnp.int32)
    for i in range(1, offsets.shape[0] - 1):
        starts = jnp.where(positions >= offsets[i], offsets[i], starts)
    return starts


def scores_of(keys, query):
    return lax.dot_general(keys, query, (((1,), (1,)), ((), ())), preferred_element_type=jnp.float32)


def visible_keys(starts, key_start, rows, first):
    key_pos = key_start + lax.broadcasted_iota(jnp.int32, (rows, 1), 0)
    visible = key_pos >= starts
    if first is not None:
        visible = visible & (key_pos <= first + lax.broadcasted_iota(jnp.int32, (1, rows), 1))
    return visible


def score_block(q_ref, k_ref, visible, before):
    factor = HEAD_DIM ** -0.5 * LOG2E
    heads = q_ref.shape[1] // HEAD_DIM
    each = heads // (k_ref.shape[1] // HEAD_DIM)
    groups = [h // each for h in range(heads)]
    scores = [
        scores_of(k_ref[:, g * HEAD_DIM : (g + 1) * HEAD_DIM], q_ref[:, h * HEAD_DIM : (h + 1) * HEAD_DIM])
        for h, g in enumerate(groups)
    ]
    scores = [jnp.where(visible, s, masked_score) for s in scores]
    tops = [jnp.max(s, axis=0, keepdims=True) for s in scores]
    if before is not None:
        olds = [before[0][h : h + 1, :] for h in range(heads)]
        tops = [jnp.maximum(old, top) for old, top in zip(olds, tops)]
    weights = [jnp.exp2((s - top) * factor) for s, top in zip(scores, tops)]
    totals = [jnp.sum(w, axis=0, keepdims=True) for w in weights]
    weights = [w.astype(jnp.bfloat16) for w in weights]
    if before is None:
        return tops, totals, weights, None
    alphas = [jnp.exp2((old - top) * factor) for old, top in zip(olds, tops)]
    totals = [before[1][h : h + 1, :] * alphas[h] + totals[h] for h in range(heads)]
    return tops, totals, weights, alphas


def value_block(v_ref, weights, alphas, acc_ref):
    groups = v_ref.shape[1] // HEAD_DIM
    each = len(weights) // groups
    values = [v_ref[:, g * HEAD_DIM : (g + 1) * HEAD_DIM].T for g in range(groups)]
    sums = [jnp.dot(values[h // each], w, preferred_element_type=jnp.float32) for h, w in enumerate(weights)]
    if alphas is None:
        return sums
    return [acc_ref[h] * alphas[h] + s for h, s in enumerate(sums)]


def store_rows(ref, rows):
    for h, row in enumerate(rows):
        ref[h : h + 1, :] = row


def state_shapes(heads, rows):
    return [
        jax.ShapeDtypeStruct((heads, rows), jnp.float32),
        jax.ShapeDtypeStruct((heads, rows), jnp.float32),
        jax.ShapeDtypeStruct((heads, HEAD_DIM, rows), jnp.float32),
    ]


def first_row(rows):
    return lax.axis_index("ctx") * rows


def reach_call(offsets, rows):
    def kernel(offsets_ref, far_ref):
        far = jnp.int32(0)
        for i in range(offsets_ref.shape[0] - 1):
            steps = (offsets_ref[i + 1] - 1) // (2 * rows) - offsets_ref[i] // (2 * rows)
            far = jnp.maximum(far, jnp.where(steps >= 2, 1, 0))
        far_ref[0] = far

    return pl.pallas_call(
        kernel,
        out_shape=jax.ShapeDtypeStruct((1,), jnp.int32),
        in_specs=[smem],
        out_specs=smem,
        name="reach",
    )(in_hbm(offsets))


def own_call(offsets, q, keys, values):
    rows, width = q.shape

    def kernel(offsets_ref, q_in, k_in, v_in, starts_ref, q_ref, k_ref, v_ref, top_ref, total_ref, acc_ref, sems):
        copies = [
            pltpu.make_async_copy(source, target, sems.at[i])
            for i, (source, target) in enumerate(((k_in, k_ref), (q_in, q_ref), (v_in, v_ref)))
        ]
        for copy in copies:
            copy.start()
        first = first_row(rows)
        starts = document_starts(offsets_ref, first, rows)
        starts_ref[...] = starts
        visible = visible_keys(starts, first, rows, first)
        for copy in copies:
            copy.wait()
        tops, totals, weights, _ = score_block(q_ref, k_ref, visible, None)
        store_rows(top_ref, tops)
        store_rows(total_ref, totals)
        for h, out in enumerate(value_block(v_ref, weights, None, None)):
            acc_ref[h] = out

    outs = pl.pallas_call(
        kernel,
        out_shape=[
            jax.ShapeDtypeStruct((1, rows), jnp.int32),
            *[jax.ShapeDtypeStruct(x.shape, x.dtype) for x in (q, keys, values)],
            *state_shapes(width // HEAD_DIM, rows),
        ],
        in_specs=[smem] + [hbm] * 3,
        out_specs=[vmem] * 7,
        scratch_shapes=[pltpu.SemaphoreType.DMA((3,))],
        compiler_params=params(),
        cost_estimate=cost(width, rows, 1),
        name="own",
    )(*[in_hbm(x) for x in (offsets, q, keys, values)])
    return outs[:4], outs[4:]


def cost(width, rows, blocks):
    return pl.CostEstimate(flops=20 * width * rows * rows * blocks, bytes_accessed=0, transcendentals=0)


def attend_call(starts, q, pieces, state):
    rows, width = q.shape
    n = len(pieces)

    def kernel(starts_ref, q_ref, *refs):
        before, after = refs[2 * n : 2 * n + 3], refs[2 * n + 3 :]
        for i, (_, _, back) in enumerate(pieces):
            k_ref, v_ref = refs[2 * i : 2 * i + 2]
            position = lax.axis_index("ctx")
            key_start = (position - back(lax.rem(position, 2))) * rows
            visible = visible_keys(starts_ref[...], key_start, rows, first_row(rows))
            source = before if i == 0 else after
            tops, totals, weights, alphas = score_block(q_ref, k_ref, visible, source)
            store_rows(after[0], tops)
            store_rows(after[1], totals)
            for h, out in enumerate(value_block(v_ref, weights, alphas, source[2])):
                after[2][h] = out

    first = 2 + 2 * n
    return pl.pallas_call(
        kernel,
        out_shape=state_shapes(width // HEAD_DIM, rows),
        in_specs=[vmem] * (first + 3),
        out_specs=[vmem] * 3,
        input_output_aliases={first + i: i for i in range(3)},
        compiler_params=params(),
        cost_estimate=cost(width, rows, n),
        name="attend",
    )(*in_vmem([starts, q, *[a for p in pieces for a in p[:2]], *state]))


def last_scores_call(starts, q, keys, back, state):
    rows, width = q.shape
    heads = width // HEAD_DIM

    def kernel(starts_ref, q_ref, k_ref, top_ref, old_total_ref, total_ref, alpha_ref, weights_ref):
        position = lax.axis_index("ctx")
        key_start = (position - back(lax.rem(position, 2))) * rows
        visible = visible_keys(starts_ref[...], key_start, rows, None)
        _, totals, weights, alphas = score_block(q_ref, k_ref, visible, (top_ref, old_total_ref))
        store_rows(total_ref, totals)
        store_rows(alpha_ref, alphas)
        for h, w in enumerate(weights):
            weights_ref[h] = w

    return pl.pallas_call(
        kernel,
        out_shape=[
            jax.ShapeDtypeStruct((heads, rows), jnp.float32),
            jax.ShapeDtypeStruct((heads, rows), jnp.float32),
            jax.ShapeDtypeStruct((heads, rows, rows), jnp.bfloat16),
        ],
        in_specs=[vmem] * 5,
        out_specs=[vmem] * 3,
        compiler_params=params(),
        cost_estimate=cost(width, rows, 1),
        name="last_scores",
    )(*in_vmem([starts, q, keys, state[0], state[1]]))


def project_into(out_ref, att_ref, w_ref, added_ref, far_core, far_next, part, parts):
    size = out_ref.shape[2]
    block = size * parts
    added_start = 0 if added_ref is None or added_ref.shape[2] == size else part * size
    step = min(size, 256)
    me = lax.axis_index("head")
    bits = (me % 2 + far_core) % 2 + 2 * ((me // 2 + far_next) % 2)
    first = pl.multiple_of(bits * block, block)
    for i in range(out_ref.shape[0]):
        for start in range(0, size, step):
            cut = slice(start, start + step)
            columns = w_ref[:, pl.ds(first + 4 * i * block + part * size + start, step)]
            value = jnp.dot(att_ref[...], columns, preferred_element_type=jnp.float32)
            if added_ref is not None:
                value = value + added_ref[i, :, added_start + start : added_start + start + step].astype(jnp.float32)
            out_ref[i, :, cut] = value.astype(out_ref.dtype)


def finish_call(values, weights, totals, alphas, acc, out_weight, count):
    heads, _, rows = acc.shape
    size = out_weight.shape[1] // count // PARTS

    def kernel(v_ref, p_ref, total_ref, alpha_ref, acc_ref, w_ref, att_ref, far_ref):
        scales = [alpha_ref[h : h + 1, :] for h in range(heads)]
        outs = value_block(v_ref, [p_ref[h] for h in range(heads)], scales, acc_ref)
        for h, out in enumerate(outs):
            head = out * (1.0 / total_ref[h : h + 1, :])
            att_ref[:, h * HEAD_DIM : (h + 1) * HEAD_DIM] = head.T.astype(jnp.bfloat16)
        project_into(far_ref, att_ref, w_ref, None, 1, 1, 0, PARTS)

    return pl.pallas_call(
        kernel,
        out_shape=[
            jax.ShapeDtypeStruct((rows, heads * HEAD_DIM), jnp.bfloat16),
            jax.ShapeDtypeStruct((count // 4, rows, size), jnp.bfloat16),
        ],
        in_specs=[vmem] * 6,
        out_specs=[vmem] * 2,
        compiler_params=params(),
        name="finish",
    )(*in_vmem([values, weights, totals, alphas, acc]), out_weight)


def rest_call(attended, out_weight, count):
    rows, depth = attended.shape
    block = out_weight.shape[1] // count

    def kernel(att_ref, w_ref, *refs):
        for part in range(1, PARTS):
            project_into(refs[part - 1], att_ref, w_ref, None, 1, 1, part, PARTS)
        project_into(refs[-1], att_ref, w_ref, None, 1, 0, 0, 1)

    sizes = [block // PARTS] * (PARTS - 1) + [block]
    return pl.pallas_call(
        kernel,
        out_shape=[jax.ShapeDtypeStruct((count // 4, rows, size), jnp.bfloat16) for size in sizes],
        in_specs=[vmem] * 2,
        out_specs=[vmem] * PARTS,
        compiler_params=params(),
        cost_estimate=pl.CostEstimate(flops=2 * rows * depth * sum(sizes) * (count // 4), bytes_accessed=0, transcendentals=0),
        name="rest",
    )(*in_vmem([attended]), out_weight)


def project_call(attended, out_weight, added, far_core, far_next, part, parts, count, out_type, name):
    rows, depth = attended.shape
    size = out_weight.shape[1] // count // parts

    def kernel(att_ref, w_ref, *refs):
        project_into(refs[-1], att_ref, w_ref, refs[0] if len(refs) > 1 else None, far_core, far_next, part, parts)

    more = [] if added is None else [added]
    return pl.pallas_call(
        kernel,
        out_shape=jax.ShapeDtypeStruct((count // 4, rows, size), out_type),
        in_specs=[vmem] * (2 + len(more)),
        out_specs=vmem,
        compiler_params=params(),
        cost_estimate=pl.CostEstimate(flops=2 * rows * depth * size * (count // 4), bytes_accessed=0, transcendentals=0),
        name=name,
    )(*in_vmem([attended]), out_weight, *in_vmem(more))


def pick_call(moving, own):
    def kernel(moving_ref, own_ref, out_ref):
        odd = lax.rem(lax.axis_index("ctx"), 2) == 1

        @pl.when(odd)
        def _():
            out_ref[...] = moving_ref[...]

        @pl.when(jnp.logical_not(odd))
        def _():
            out_ref[...] = own_ref[...]

    return pl.pallas_call(
        kernel,
        out_shape=jax.ShapeDtypeStruct(own.shape, own.dtype),
        in_specs=[vmem] * 2,
        out_specs=vmem,
        compiler_params=params(),
        name="pick",
    )(*in_vmem([moving, own]))


def output_call(kept, arrived, part, whole):
    rows, size = kept.shape

    def kernel(kept_ref, arrived_ref, *refs):
        out_ref, held, sem = refs[-3:]
        held[...] = (kept_ref[...] + arrived_ref[...].astype(jnp.float32)).T.astype(jnp.bfloat16)
        copy = pltpu.make_async_copy(held, out_ref.at[part * size : (part + 1) * size], sem)
        copy.start()
        copy.wait()

    more = [] if whole is None else [in_hbm(whole)]
    return pl.pallas_call(
        kernel,
        out_shape=jax.ShapeDtypeStruct((size * PARTS, rows), jnp.bfloat16),
        in_specs=[vmem] * 2 + [hbm] * len(more),
        out_specs=hbm,
        scratch_shapes=[pltpu.VMEM((size, rows), jnp.bfloat16), pltpu.SemaphoreType.DMA],
        input_output_aliases={2: 0} if more else {},
        compiler_params=params(),
        name="output",
    )(*in_vmem([kept, arrived]), *more)


def swapped(array, axis, bit):
    return lax.ppermute(array, axis, [(i, i ^ bit) for i in range(lax.axis_size(axis))])


def summed_over_heads(attended, far, out_weight, count):
    def project(added, far_core, far_next, part, parts, out_type, name):
        return project_call(attended, out_weight, added, far_core, far_next, part, parts, count, out_type, name)

    *fars, near = rest_call(attended, out_weight, count)
    got_fars = [swapped(x, "head", 1) for x in (far, *fars)]
    sents = [project(got_fars[part], 0, 1, part, PARTS, jnp.bfloat16, "sent") for part in range(PARTS)]
    gots = [swapped(x, "head", 2) for x in sents]
    got_near = swapped(near, "head", 1)
    kepts = [project(got_near, 0, 0, part, PARTS, jnp.float32, "kept") for part in range(PARTS)]
    me = lax.axis_index("head")
    whole = None
    for part, (kept, got) in enumerate(zip(kepts, gots)):
        for b in range(2, count.bit_length() - 1):
            kept = kept + got.astype(jnp.float32)
            pairs = kept.reshape(kept.shape[0] // 2, 2, *kept.shape[1:])
            bit = (me >> b) & 1
            sent = lax.dynamic_index_in_dim(pairs, 1 - bit, 1, keepdims=False)
            kept = lax.dynamic_index_in_dim(pairs, bit, 1, keepdims=False)
            got = swapped(sent.astype(jnp.bfloat16), "head", 1 << b)
        whole = output_call(kept[0], got[0], part, whole)
    return whole


def on_device(queries, key_vectors, value_vectors, out_weight, offsets):
    devices = lax.axis_size("ctx")
    heads = lax.axis_size("head")
    rows = queries.shape[0]
    pair_steps = (min(REACH, devices // 2) + 1) // 2

    def shifted(pair):
        return tuple(lax.ppermute(m, "ctx", [(i, (i + 2) % devices) for i in range(devices)]) for m in pair)

    def across(pair):
        return tuple(swapped(m, "ctx", 1) for m in pair)

    def after(pair, state):
        first, state = lax.optimization_barrier((pair[0], state))
        return (first, pair[1]), state

    def finished(starts, q, pair, back, state, out_weight):
        totals, alphas, weights = last_scores_call(starts, q, pair[0], back, state)
        attended, product = finish_call(pair[1], weights, totals, alphas, state[2], out_weight, heads)
        return summed_over_heads(attended, product, out_weight, heads)

    def near(queries, key_vectors, value_vectors, out_weight, offsets):
        moved = shifted((key_vectors, value_vectors))
        beside = across((key_vectors, value_vectors))
        (starts, q, _, _), state = own_call(offsets, queries, key_vectors, value_vectors)
        moved, state = after(moved, state)
        crossed = across(moved)
        state = attend_call(starts, q, [(*moved, lambda x: 2), (*beside, lambda x: 2 * x - 1)], state)
        return finished(starts, q, crossed, lambda x: 1 + 2 * x, state, out_weight)

    def reaching(queries, key_vectors, value_vectors, out_weight, offsets):
        moved = (key_vectors, value_vectors)
        (starts, q, keys, values), state = own_call(offsets, queries, key_vectors, value_vectors)
        waiting = []
        for step in range(1, pair_steps + 1):
            moved, state = after(shifted(moved), state)
            waiting.append((*moved, lambda x, step=step: 2 * step))
            if step < pair_steps:
                crossed = across(moved)
                state = attend_call(starts, q, waiting, state)
                waiting = [(*crossed, lambda x, step=step: 2 * step - 1 + 2 * x)]
        crossed = across([pick_call(m, o) for m, o in zip(moved, (keys, values))])
        state = attend_call(starts, q, waiting, state)
        return finished(starts, q, crossed, lambda x: jnp.where(x == 1, 1, 2 * pair_steps - 1), state, out_weight)

    given = (queries, key_vectors, value_vectors, out_weight, offsets)
    if pair_steps == 1:
        return near(*given)
    return lax.cond(reach_call(offsets, rows)[0] > 0, reaching, near, *given)


def solution(mesh):
    placed = (P("ctx", "head"), P("ctx", "head"), P("ctx", "head"), P("head", None), P())
    return jax.shard_map(
        on_device, mesh=mesh, in_specs=placed, out_specs=P("head", "ctx"), check_vma=False
    )
```

```python
import jax
import jax.numpy as jnp
from jax import lax
from jax.experimental import pallas as pl
from jax.experimental.pallas import tpu as pltpu
from jax.sharding import PartitionSpec as P

HEAD_DIM = 128
REACH = 15
LOG2E = 1.4426950408889634
masked_score = -1e30
PARTS = 2
VMEM_LIMIT = 20 * 1024 * 1024

vmem = pl.BlockSpec(memory_space=pltpu.VMEM)
smem = pl.BlockSpec(memory_space=pltpu.SMEM)
hbm = pl.BlockSpec(memory_space=pltpu.HBM)


def in_hbm(array):
    return pltpu.with_memory_space_constraint(array, pltpu.HBM)


def in_vmem(arrays):
    return [pltpu.with_memory_space_constraint(a, pltpu.VMEM) for a in arrays]


def params():
    return pltpu.CompilerParams(vmem_limit_bytes=VMEM_LIMIT)


def document_starts(offsets, first, rows):
    positions = first + lax.broadcasted_iota(jnp.int32, (1, rows), 1)
    starts = jnp.zeros((1, rows), jnp.int32)
    for i in range(1, offsets.shape[0] - 1):
        starts = jnp.where(positions >= offsets[i], offsets[i], starts)
    return starts


def scores_of(keys, query):
    return lax.dot_general(keys, query, (((1,), (1,)), ((), ())), preferred_element_type=jnp.float32)


def visible_keys(starts, key_start, rows, first):
    key_pos = key_start + lax.broadcasted_iota(jnp.int32, (rows, 1), 0)
    visible = key_pos >= starts
    if first is not None:
        visible = visible & (key_pos <= first + lax.broadcasted_iota(jnp.int32, (1, rows), 1))
    return visible


def score_block(q_ref, k_ref, visible, before):
    factor = HEAD_DIM ** -0.5 * LOG2E
    heads = q_ref.shape[1] // HEAD_DIM
    each = heads // (k_ref.shape[1] // HEAD_DIM)
    groups = [h // each for h in range(heads)]
    scores = [
        scores_of(k_ref[:, g * HEAD_DIM : (g + 1) * HEAD_DIM], q_ref[:, h * HEAD_DIM : (h + 1) * HEAD_DIM])
        for h, g in enumerate(groups)
    ]
    scores = [jnp.where(visible, s, masked_score) for s in scores]
    tops = [jnp.max(s, axis=0, keepdims=True) for s in scores]
    if before is not None:
        olds = [before[0][h : h + 1, :] for h in range(heads)]
        tops = [jnp.maximum(old, top) for old, top in zip(olds, tops)]
    weights = [jnp.exp2((s - top) * factor) for s, top in zip(scores, tops)]
    totals = [jnp.sum(w, axis=0, keepdims=True) for w in weights]
    weights = [w.astype(jnp.bfloat16) for w in weights]
    if before is None:
        return tops, totals, weights, None
    alphas = [jnp.exp2((old - top) * factor) for old, top in zip(olds, tops)]
    totals = [before[1][h : h + 1, :] * alphas[h] + totals[h] for h in range(heads)]
    return tops, totals, weights, alphas


def value_block(v_ref, weights, alphas, acc_ref):
    groups = v_ref.shape[1] // HEAD_DIM
    each = len(weights) // groups
    values = [v_ref[:, g * HEAD_DIM : (g + 1) * HEAD_DIM].T for g in range(groups)]
    sums = [jnp.dot(values[h // each], w, preferred_element_type=jnp.float32) for h, w in enumerate(weights)]
    if alphas is None:
        return sums
    return [acc_ref[h] * alphas[h] + s for h, s in enumerate(sums)]


def store_rows(ref, rows):
    for h, row in enumerate(rows):
        ref[h : h + 1, :] = row


def state_shapes(heads, rows):
    return [
        jax.ShapeDtypeStruct((heads, rows), jnp.float32),
        jax.ShapeDtypeStruct((heads, rows), jnp.float32),
        jax.ShapeDtypeStruct((heads, HEAD_DIM, rows), jnp.float32),
    ]


def first_row(rows):
    return lax.axis_index("ctx") * rows


def reach_call(offsets, rows):
    def kernel(offsets_ref, far_ref):
        far = jnp.int32(0)
        for i in range(offsets_ref.shape[0] - 1):
            steps = (offsets_ref[i + 1] - 1) // (2 * rows) - offsets_ref[i] // (2 * rows)
            far = jnp.maximum(far, jnp.where(steps >= 2, 1, 0))
        far_ref[0] = far

    return pl.pallas_call(
        kernel,
        out_shape=pltpu.SMEM((1,), jnp.int32),
        in_specs=[smem],
        out_specs=smem,
        name="reach",
    )(in_hbm(offsets))


def own_call(offsets, q, keys, values):
    rows, width = q.shape

    def kernel(offsets_ref, q_in, k_in, v_in, starts_ref, q_ref, k_ref, v_ref, top_ref, total_ref, acc_ref, sems):
        copies = [
            pltpu.make_async_copy(source, target, sems.at[i])
            for i, (source, target) in enumerate(((k_in, k_ref), (q_in, q_ref), (v_in, v_ref)))
        ]
        for copy in copies:
            copy.start()
        first = first_row(rows)
        starts = document_starts(offsets_ref, first, rows)
        starts_ref[...] = starts
        visible = visible_keys(starts, first, rows, first)
        for copy in copies:
            copy.wait()
        tops, totals, weights, _ = score_block(q_ref, k_ref, visible, None)
        store_rows(top_ref, tops)
        store_rows(total_ref, totals)
        for h, out in enumerate(value_block(v_ref, weights, None, None)):
            acc_ref[h] = out

    outs = pl.pallas_call(
        kernel,
        out_shape=[
            jax.ShapeDtypeStruct((1, rows), jnp.int32),
            *[jax.ShapeDtypeStruct(x.shape, x.dtype) for x in (q, keys, values)],
            *state_shapes(width // HEAD_DIM, rows),
        ],
        in_specs=[smem] + [hbm] * 3,
        out_specs=[vmem] * 7,
        scratch_shapes=[pltpu.SemaphoreType.DMA((3,))],
        compiler_params=params(),
        cost_estimate=cost(width, rows, 1),
        name="own",
    )(*[in_hbm(x) for x in (offsets, q, keys, values)])
    return outs[:4], outs[4:]


def cost(width, rows, blocks):
    return pl.CostEstimate(flops=20 * width * rows * rows * blocks, bytes_accessed=0, transcendentals=0)


def attend_call(starts, q, pieces, state):
    rows, width = q.shape
    n = len(pieces)

    def kernel(starts_ref, q_ref, *refs):
        before, after = refs[2 * n : 2 * n + 3], refs[2 * n + 3 :]
        for i, (_, _, back) in enumerate(pieces):
            k_ref, v_ref = refs[2 * i : 2 * i + 2]
            position = lax.axis_index("ctx")
            key_start = (position - back(lax.rem(position, 2))) * rows
            visible = visible_keys(starts_ref[...], key_start, rows, first_row(rows))
            source = before if i == 0 else after
            tops, totals, weights, alphas = score_block(q_ref, k_ref, visible, source)
            store_rows(after[0], tops)
            store_rows(after[1], totals)
            for h, out in enumerate(value_block(v_ref, weights, alphas, source[2])):
                after[2][h] = out

    first = 2 + 2 * n
    return pl.pallas_call(
        kernel,
        out_shape=state_shapes(width // HEAD_DIM, rows),
        in_specs=[vmem] * (first + 3),
        out_specs=[vmem] * 3,
        input_output_aliases={first + i: i for i in range(3)},
        compiler_params=params(),
        cost_estimate=cost(width, rows, n),
        name="attend",
    )(*in_vmem([starts, q, *[a for p in pieces for a in p[:2]], *state]))


def last_scores_call(starts, q, keys, back, state):
    rows, width = q.shape
    heads = width // HEAD_DIM

    def kernel(starts_ref, q_ref, k_ref, top_ref, old_total_ref, total_ref, alpha_ref, weights_ref):
        position = lax.axis_index("ctx")
        key_start = (position - back(lax.rem(position, 2))) * rows
        visible = visible_keys(starts_ref[...], key_start, rows, None)
        _, totals, weights, alphas = score_block(q_ref, k_ref, visible, (top_ref, old_total_ref))
        store_rows(total_ref, totals)
        store_rows(alpha_ref, alphas)
        for h, w in enumerate(weights):
            weights_ref[h] = w

    return pl.pallas_call(
        kernel,
        out_shape=[
            jax.ShapeDtypeStruct((heads, rows), jnp.float32),
            jax.ShapeDtypeStruct((heads, rows), jnp.float32),
            jax.ShapeDtypeStruct((heads, rows, rows), jnp.bfloat16),
        ],
        in_specs=[vmem] * 5,
        out_specs=[vmem] * 3,
        compiler_params=params(),
        cost_estimate=cost(width, rows, 1),
        name="last_scores",
    )(*in_vmem([starts, q, keys, state[0], state[1]]))


def project_into(out_ref, att_ref, w_ref, added_ref, far_core, far_next, part, parts):
    size = out_ref.shape[2]
    block = size * parts
    added_start = 0 if added_ref is None or added_ref.shape[2] == size else part * size
    step = min(size, 256)
    me = lax.axis_index("head")
    bits = (me % 2 + far_core) % 2 + 2 * ((me // 2 + far_next) % 2)
    first = pl.multiple_of(bits * block, block)
    for i in range(out_ref.shape[0]):
        for start in range(0, size, step):
            cut = slice(start, start + step)
            columns = w_ref[:, pl.ds(first + 4 * i * block + part * size + start, step)]
            value = jnp.dot(att_ref[...], columns, preferred_element_type=jnp.float32)
            if added_ref is not None:
                value = value + added_ref[i, :, added_start + start : added_start + start + step].astype(jnp.float32)
            out_ref[i, :, cut] = value.astype(out_ref.dtype)


def finish_call(values, weights, totals, alphas, acc, out_weight, count):
    heads, _, rows = acc.shape
    size = out_weight.shape[1] // count // PARTS

    def kernel(v_ref, p_ref, total_ref, alpha_ref, acc_ref, w_ref, att_ref, far_ref):
        scales = [alpha_ref[h : h + 1, :] for h in range(heads)]
        outs = value_block(v_ref, [p_ref[h] for h in range(heads)], scales, acc_ref)
        for h, out in enumerate(outs):
            head = out * (1.0 / total_ref[h : h + 1, :])
            att_ref[:, h * HEAD_DIM : (h + 1) * HEAD_DIM] = head.T.astype(jnp.bfloat16)
        project_into(far_ref, att_ref, w_ref, None, 1, 1, 0, PARTS)

    return pl.pallas_call(
        kernel,
        out_shape=[
            jax.ShapeDtypeStruct((rows, heads * HEAD_DIM), jnp.bfloat16),
            jax.ShapeDtypeStruct((count // 4, rows, size), jnp.bfloat16),
        ],
        in_specs=[vmem] * 6,
        out_specs=[vmem] * 2,
        compiler_params=params(),
        name="finish",
    )(*in_vmem([values, weights, totals, alphas, acc]), out_weight)


def rest_call(attended, out_weight, count):
    rows, depth = attended.shape
    block = out_weight.shape[1] // count

    def kernel(att_ref, w_ref, *refs):
        for part in range(1, PARTS):
            project_into(refs[part - 1], att_ref, w_ref, None, 1, 1, part, PARTS)
        project_into(refs[-1], att_ref, w_ref, None, 1, 0, 0, 1)

    sizes = [block // PARTS] * (PARTS - 1) + [block]
    return pl.pallas_call(
        kernel,
        out_shape=[jax.ShapeDtypeStruct((count // 4, rows, size), jnp.bfloat16) for size in sizes],
        in_specs=[vmem] * 2,
        out_specs=[vmem] * PARTS,
        compiler_params=params(),
        cost_estimate=pl.CostEstimate(flops=2 * rows * depth * sum(sizes) * (count // 4), bytes_accessed=0, transcendentals=0),
        name="rest",
    )(*in_vmem([attended]), out_weight)


def project_call(attended, out_weight, added, far_core, far_next, part, parts, count, out_type, name):
    rows, depth = attended.shape
    size = out_weight.shape[1] // count // parts

    def kernel(att_ref, w_ref, *refs):
        project_into(refs[-1], att_ref, w_ref, refs[0] if len(refs) > 1 else None, far_core, far_next, part, parts)

    more = [] if added is None else [added]
    return pl.pallas_call(
        kernel,
        out_shape=jax.ShapeDtypeStruct((count // 4, rows, size), out_type),
        in_specs=[vmem] * (2 + len(more)),
        out_specs=vmem,
        compiler_params=params(),
        cost_estimate=pl.CostEstimate(flops=2 * rows * depth * size * (count // 4), bytes_accessed=0, transcendentals=0),
        name=name,
    )(*in_vmem([attended]), out_weight, *in_vmem(more))


def pick_call(moving, own):
    def kernel(moving_ref, own_ref, out_ref):
        odd = lax.rem(lax.axis_index("ctx"), 2) == 1

        @pl.when(odd)
        def _():
            out_ref[...] = moving_ref[...]

        @pl.when(jnp.logical_not(odd))
        def _():
            out_ref[...] = own_ref[...]

    return pl.pallas_call(
        kernel,
        out_shape=jax.ShapeDtypeStruct(own.shape, own.dtype),
        in_specs=[vmem] * 2,
        out_specs=vmem,
        compiler_params=params(),
        name="pick",
    )(*in_vmem([moving, own]))


def output_call(kept, arrived, part, whole):
    rows, size = kept.shape

    def kernel(kept_ref, arrived_ref, *refs):
        out_ref, held, sem = refs[-3:]
        held[...] = (kept_ref[...] + arrived_ref[...].astype(jnp.float32)).T.astype(jnp.bfloat16)
        copy = pltpu.make_async_copy(held, out_ref.at[part * size : (part + 1) * size], sem)
        copy.start()
        copy.wait()

    more = [] if whole is None else [in_hbm(whole)]
    return pl.pallas_call(
        kernel,
        out_shape=jax.ShapeDtypeStruct((size * PARTS, rows), jnp.bfloat16),
        in_specs=[vmem] * 2 + [hbm] * len(more),
        out_specs=hbm,
        scratch_shapes=[pltpu.VMEM((size, rows), jnp.bfloat16), pltpu.SemaphoreType.DMA],
        input_output_aliases={2: 0} if more else {},
        compiler_params=params(),
        name="output",
    )(*in_vmem([kept, arrived]), *more)


def swapped(array, axis, bit):
    return lax.ppermute(array, axis, [(i, i ^ bit) for i in range(lax.axis_size(axis))])


def summed_over_heads(attended, far, out_weight, count):
    def project(added, far_core, far_next, part, parts, out_type, name):
        return project_call(attended, out_weight, added, far_core, far_next, part, parts, count, out_type, name)

    *fars, near = rest_call(attended, out_weight, count)
    got_fars = [swapped(x, "head", 1) for x in (far, *fars)]
    sents = [project(got_fars[part], 0, 1, part, PARTS, jnp.bfloat16, "sent") for part in range(PARTS)]
    gots = [swapped(x, "head", 2) for x in sents]
    got_near = swapped(near, "head", 1)
    kepts = [project(got_near, 0, 0, part, PARTS, jnp.float32, "kept") for part in range(PARTS)]
    me = lax.axis_index("head")
    whole = None
    for part, (kept, got) in enumerate(zip(kepts, gots)):
        for b in range(2, count.bit_length() - 1):
            kept = kept + got.astype(jnp.float32)
            pairs = kept.reshape(kept.shape[0] // 2, 2, *kept.shape[1:])
            bit = (me >> b) & 1
            sent = lax.dynamic_index_in_dim(pairs, 1 - bit, 1, keepdims=False)
            kept = lax.dynamic_index_in_dim(pairs, bit, 1, keepdims=False)
            got = swapped(sent.astype(jnp.bfloat16), "head", 1 << b)
        whole = output_call(kept[0], got[0], part, whole)
    return whole


def on_device(queries, key_vectors, value_vectors, out_weight, offsets):
    devices = lax.axis_size("ctx")
    heads = lax.axis_size("head")
    rows = queries.shape[0]
    pair_steps = (min(REACH, devices // 2) + 1) // 2

    def shifted(pair):
        return tuple(lax.ppermute(m, "ctx", [(i, (i + 2) % devices) for i in range(devices)]) for m in pair)

    def across(pair):
        return tuple(swapped(m, "ctx", 1) for m in pair)

    def after(pair, state):
        first, state = lax.optimization_barrier((pair[0], state))
        return (first, pair[1]), state

    def finished(starts, q, pair, back, state, out_weight):
        totals, alphas, weights = last_scores_call(starts, q, pair[0], back, state)
        attended, product = finish_call(pair[1], weights, totals, alphas, state[2], out_weight, heads)
        return summed_over_heads(attended, product, out_weight, heads)

    def near(queries, key_vectors, value_vectors, out_weight, offsets):
        moved = shifted((key_vectors, value_vectors))
        beside = across((key_vectors, value_vectors))
        (starts, q, _, _), state = own_call(offsets, queries, key_vectors, value_vectors)
        moved, state = after(moved, state)
        crossed = across(moved)
        state = attend_call(starts, q, [(*moved, lambda x: 2)], state)
        state = attend_call(starts, q, [(*beside, lambda x: 2 * x - 1)], state)
        return finished(starts, q, crossed, lambda x: 1 + 2 * x, state, out_weight)

    def reaching(queries, key_vectors, value_vectors, out_weight, offsets):
        moved = (key_vectors, value_vectors)
        (starts, q, keys, values), state = own_call(offsets, queries, key_vectors, value_vectors)
        waiting = []
        for step in range(1, pair_steps + 1):
            moved, state = after(shifted(moved), state)
            waiting.insert(0, (*moved, lambda x, step=step: 2 * step))
            if step < pair_steps:
                crossed = across(moved)
                for piece in waiting:
                    state = attend_call(starts, q, [piece], state)
                waiting = [(*crossed, lambda x, step=step: 2 * step - 1 + 2 * x)]
        crossed = across([pick_call(m, o) for m, o in zip(moved, (keys, values))])
        for piece in waiting:
            state = attend_call(starts, q, [piece], state)
        return finished(starts, q, crossed, lambda x: jnp.where(x == 1, 1, 2 * pair_steps - 1), state, out_weight)

    given = (queries, key_vectors, value_vectors, out_weight, offsets)
    if pair_steps == 1:
        return near(*given)
    return lax.cond(reach_call(offsets, rows)[0] > 0, reaching, near, *given)


def solution(mesh):
    placed = (P("ctx", "head"), P("ctx", "head"), P("ctx", "head"), P("head", None), P())
    return jax.shard_map(
        on_device, mesh=mesh, in_specs=placed, out_specs=P("head", "ctx"), check_vma=False
    )
```

```python
import jax
import jax.numpy as jnp
from jax import lax
from jax.experimental import pallas as pl
from jax.experimental.pallas import tpu as pltpu
from jax.sharding import PartitionSpec as P

HEAD_DIM = 128
REACH = 15
LOG2E = 1.4426950408889634
masked_score = -1e30
PARTS = 2
VMEM_LIMIT = 20 * 1024 * 1024

vmem = pl.BlockSpec(memory_space=pltpu.VMEM)
smem = pl.BlockSpec(memory_space=pltpu.SMEM)
hbm = pl.BlockSpec(memory_space=pltpu.HBM)


def in_hbm(array):
    return pltpu.with_memory_space_constraint(array, pltpu.HBM)


def in_vmem(arrays):
    return [pltpu.with_memory_space_constraint(a, pltpu.VMEM) for a in arrays]


def params():
    return pltpu.CompilerParams(vmem_limit_bytes=VMEM_LIMIT)


def document_starts(offsets, first, rows):
    positions = first + lax.broadcasted_iota(jnp.int32, (1, rows), 1)
    starts = jnp.zeros((1, rows), jnp.int32)
    for i in range(1, offsets.shape[0] - 1):
        starts = jnp.where(positions >= offsets[i], offsets[i], starts)
    return starts


def scores_of(keys, query):
    return lax.dot_general(keys, query, (((1,), (1,)), ((), ())), preferred_element_type=jnp.float32)


def visible_keys(starts, key_start, rows, first):
    key_pos = key_start + lax.broadcasted_iota(jnp.int32, (rows, 1), 0)
    visible = key_pos >= starts
    if first is not None:
        visible = visible & (key_pos <= first + lax.broadcasted_iota(jnp.int32, (1, rows), 1))
    return visible


def score_block(q_ref, k_ref, visible, before):
    factor = HEAD_DIM ** -0.5 * LOG2E
    heads = q_ref.shape[1] // HEAD_DIM
    each = heads // (k_ref.shape[1] // HEAD_DIM)
    groups = [h // each for h in range(heads)]
    scores = [
        scores_of(k_ref[:, g * HEAD_DIM : (g + 1) * HEAD_DIM], q_ref[:, h * HEAD_DIM : (h + 1) * HEAD_DIM])
        for h, g in enumerate(groups)
    ]
    scores = [jnp.where(visible, s, masked_score) for s in scores]
    tops = [jnp.max(s, axis=0, keepdims=True) for s in scores]
    if before is not None:
        olds = [before[0][h : h + 1, :] for h in range(heads)]
        tops = [jnp.maximum(old, top) for old, top in zip(olds, tops)]
    weights = [jnp.exp2((s - top) * factor) for s, top in zip(scores, tops)]
    totals = [jnp.sum(w, axis=0, keepdims=True) for w in weights]
    weights = [w.astype(jnp.bfloat16) for w in weights]
    if before is None:
        return tops, totals, weights, None
    alphas = [jnp.exp2((old - top) * factor) for old, top in zip(olds, tops)]
    totals = [before[1][h : h + 1, :] * alphas[h] + totals[h] for h in range(heads)]
    return tops, totals, weights, alphas


def value_block(v_ref, weights, alphas, acc_ref):
    groups = v_ref.shape[1] // HEAD_DIM
    each = len(weights) // groups
    values = [v_ref[:, g * HEAD_DIM : (g + 1) * HEAD_DIM].T for g in range(groups)]
    sums = [jnp.dot(values[h // each], w, preferred_element_type=jnp.float32) for h, w in enumerate(weights)]
    if alphas is None:
        return sums
    return [acc_ref[h] * alphas[h] + s for h, s in enumerate(sums)]


def store_rows(ref, rows):
    for h, row in enumerate(rows):
        ref[h : h + 1, :] = row


def state_shapes(heads, rows):
    return [
        jax.ShapeDtypeStruct((heads, rows), jnp.float32),
        jax.ShapeDtypeStruct((heads, rows), jnp.float32),
        jax.ShapeDtypeStruct((heads, HEAD_DIM, rows), jnp.float32),
    ]


def first_row(rows):
    return lax.axis_index("ctx") * rows


def reach_call(offsets, rows):
    def kernel(offsets_ref, far_ref):
        far = jnp.int32(0)
        for i in range(offsets_ref.shape[0] - 1):
            steps = (offsets_ref[i + 1] - 1) // (2 * rows) - offsets_ref[i] // (2 * rows)
            far = jnp.maximum(far, jnp.where(steps >= 2, 1, 0))
        far_ref[0] = far

    return pl.pallas_call(
        kernel,
        out_shape=pltpu.SMEM((1,), jnp.int32),
        in_specs=[smem],
        out_specs=smem,
        name="reach",
    )(in_hbm(offsets))


def own_call(offsets, q, keys, values):
    rows, width = q.shape

    def kernel(offsets_ref, q_in, k_in, v_in, starts_ref, q_ref, top_ref, total_ref, acc_ref, k_ref, v_ref, sems):
        copies = [
            pltpu.make_async_copy(source, target, sems.at[i])
            for i, (source, target) in enumerate(((k_in, k_ref), (q_in, q_ref), (v_in, v_ref)))
        ]
        for copy in copies:
            copy.start()
        first = first_row(rows)
        starts = document_starts(offsets_ref, first, rows)
        starts_ref[...] = starts
        visible = visible_keys(starts, first, rows, first)
        for copy in copies:
            copy.wait()
        tops, totals, weights, _ = score_block(q_ref, k_ref, visible, None)
        store_rows(top_ref, tops)
        store_rows(total_ref, totals)
        for h, out in enumerate(value_block(v_ref, weights, None, None)):
            acc_ref[h] = out

    outs = pl.pallas_call(
        kernel,
        out_shape=[
            jax.ShapeDtypeStruct((1, rows), jnp.int32),
            jax.ShapeDtypeStruct(q.shape, q.dtype),
            *state_shapes(width // HEAD_DIM, rows),
        ],
        in_specs=[smem] + [hbm] * 3,
        out_specs=[vmem] * 5,
        scratch_shapes=[pltpu.VMEM(x.shape, x.dtype) for x in (keys, values)] + [pltpu.SemaphoreType.DMA((3,))],
        compiler_params=params(),
        cost_estimate=cost(width, rows, 1),
        name="own",
    )(*[in_hbm(x) for x in (offsets, q, keys, values)])
    return *outs[:2], outs[2:]


def cost(width, rows, blocks):
    return pl.CostEstimate(flops=20 * width * rows * rows * blocks, bytes_accessed=0, transcendentals=0)


def attend_call(starts, q, pieces, state):
    rows, width = q.shape
    n = len(pieces)

    def kernel(starts_ref, q_ref, *refs):
        before, after = refs[2 * n : 2 * n + 3], refs[2 * n + 3 :]
        for i, (_, _, back) in enumerate(pieces):
            k_ref, v_ref = refs[2 * i : 2 * i + 2]
            position = lax.axis_index("ctx")
            key_start = (position - back(lax.rem(position, 2))) * rows
            visible = visible_keys(starts_ref[...], key_start, rows, first_row(rows))
            source = before if i == 0 else after
            tops, totals, weights, alphas = score_block(q_ref, k_ref, visible, source)
            store_rows(after[0], tops)
            store_rows(after[1], totals)
            for h, out in enumerate(value_block(v_ref, weights, alphas, source[2])):
                after[2][h] = out

    first = 2 + 2 * n
    return pl.pallas_call(
        kernel,
        out_shape=state_shapes(width // HEAD_DIM, rows),
        in_specs=[vmem] * (first + 3),
        out_specs=[vmem] * 3,
        input_output_aliases={first + i: i for i in range(3)},
        compiler_params=params(),
        cost_estimate=cost(width, rows, n),
        name="attend",
    )(*in_vmem([starts, q, *[a for p in pieces for a in p[:2]], *state]))


def last_scores_call(starts, q, keys, back, state):
    rows, width = q.shape
    heads = width // HEAD_DIM

    def kernel(starts_ref, q_ref, k_ref, top_ref, old_total_ref, total_ref, alpha_ref, weights_ref):
        position = lax.axis_index("ctx")
        key_start = (position - back(lax.rem(position, 2))) * rows
        visible = visible_keys(starts_ref[...], key_start, rows, None)
        _, totals, weights, alphas = score_block(q_ref, k_ref, visible, (top_ref, old_total_ref))
        store_rows(total_ref, totals)
        store_rows(alpha_ref, alphas)
        for h, w in enumerate(weights):
            weights_ref[h] = w

    return pl.pallas_call(
        kernel,
        out_shape=[
            jax.ShapeDtypeStruct((heads, rows), jnp.float32),
            jax.ShapeDtypeStruct((heads, rows), jnp.float32),
            jax.ShapeDtypeStruct((heads, rows, rows), jnp.bfloat16),
        ],
        in_specs=[vmem] * 5,
        out_specs=[vmem] * 3,
        compiler_params=params(),
        cost_estimate=cost(width, rows, 1),
        name="last_scores",
    )(*in_vmem([starts, q, keys, state[0], state[1]]))


def project_into(out_ref, att_ref, w_ref, added_ref, far_core, far_next, part, parts):
    size = out_ref.shape[2]
    block = size * parts
    added_start = 0 if added_ref is None or added_ref.shape[2] == size else part * size
    step = min(size, 256)
    me = lax.axis_index("head")
    bits = (me % 2 + far_core) % 2 + 2 * ((me // 2 + far_next) % 2)
    first = pl.multiple_of(bits * block, block)
    for i in range(out_ref.shape[0]):
        for start in range(0, size, step):
            cut = slice(start, start + step)
            columns = w_ref[:, pl.ds(first + 4 * i * block + part * size + start, step)]
            value = jnp.dot(att_ref[...], columns, preferred_element_type=jnp.float32)
            if added_ref is not None:
                value = value + added_ref[i, :, added_start + start : added_start + start + step].astype(jnp.float32)
            out_ref[i, :, cut] = value.astype(out_ref.dtype)


def finish_call(values, weights, totals, alphas, acc, out_weight, count):
    heads, _, rows = acc.shape
    size = out_weight.shape[1] // count // PARTS

    def kernel(v_ref, p_ref, total_ref, alpha_ref, acc_ref, w_ref, att_ref, far_ref):
        scales = [alpha_ref[h : h + 1, :] for h in range(heads)]
        outs = value_block(v_ref, [p_ref[h] for h in range(heads)], scales, acc_ref)
        for h, out in enumerate(outs):
            head = out * (1.0 / total_ref[h : h + 1, :])
            att_ref[:, h * HEAD_DIM : (h + 1) * HEAD_DIM] = head.T.astype(jnp.bfloat16)
        project_into(far_ref, att_ref, w_ref, None, 1, 1, 0, PARTS)

    return pl.pallas_call(
        kernel,
        out_shape=[
            jax.ShapeDtypeStruct((rows, heads * HEAD_DIM), jnp.bfloat16),
            jax.ShapeDtypeStruct((count // 4, rows, size), jnp.bfloat16),
        ],
        in_specs=[vmem] * 6,
        out_specs=[vmem] * 2,
        compiler_params=params(),
        name="finish",
    )(*in_vmem([values, weights, totals, alphas, acc]), out_weight)


def rest_call(attended, out_weight, count):
    rows, depth = attended.shape
    block = out_weight.shape[1] // count

    def kernel(att_ref, w_ref, *refs):
        for part in range(1, PARTS):
            project_into(refs[part - 1], att_ref, w_ref, None, 1, 1, part, PARTS)
        project_into(refs[-1], att_ref, w_ref, None, 1, 0, 0, 1)

    sizes = [block // PARTS] * (PARTS - 1) + [block]
    return pl.pallas_call(
        kernel,
        out_shape=[jax.ShapeDtypeStruct((count // 4, rows, size), jnp.bfloat16) for size in sizes],
        in_specs=[vmem] * 2,
        out_specs=[vmem] * PARTS,
        compiler_params=params(),
        cost_estimate=pl.CostEstimate(flops=2 * rows * depth * sum(sizes) * (count // 4), bytes_accessed=0, transcendentals=0),
        name="rest",
    )(*in_vmem([attended]), out_weight)


def project_call(attended, out_weight, added, far_core, far_next, part, parts, count, out_type, name):
    rows, depth = attended.shape
    size = out_weight.shape[1] // count // parts

    def kernel(att_ref, w_ref, *refs):
        project_into(refs[-1], att_ref, w_ref, refs[0] if len(refs) > 1 else None, far_core, far_next, part, parts)

    more = [] if added is None else [added]
    return pl.pallas_call(
        kernel,
        out_shape=jax.ShapeDtypeStruct((count // 4, rows, size), out_type),
        in_specs=[vmem] * (2 + len(more)),
        out_specs=vmem,
        compiler_params=params(),
        cost_estimate=pl.CostEstimate(flops=2 * rows * depth * size * (count // 4), bytes_accessed=0, transcendentals=0),
        name=name,
    )(*in_vmem([attended]), out_weight, *in_vmem(more))


def output_call(kept, arrived, part, whole):
    rows, size = kept.shape

    def kernel(kept_ref, arrived_ref, *refs):
        out_ref, held, sem = refs[-3:]
        held[...] = (kept_ref[...] + arrived_ref[...].astype(jnp.float32)).T.astype(jnp.bfloat16)
        copy = pltpu.make_async_copy(held, out_ref.at[part * size : (part + 1) * size], sem)
        copy.start()
        copy.wait()

    more = [] if whole is None else [in_hbm(whole)]
    return pl.pallas_call(
        kernel,
        out_shape=jax.ShapeDtypeStruct((size * PARTS, rows), jnp.bfloat16),
        in_specs=[vmem] * 2 + [hbm] * len(more),
        out_specs=hbm,
        scratch_shapes=[pltpu.VMEM((size, rows), jnp.bfloat16), pltpu.SemaphoreType.DMA],
        input_output_aliases={2: 0} if more else {},
        compiler_params=params(),
        name="output",
    )(*in_vmem([kept, arrived]), *more)


def swapped(array, axis, bit):
    return lax.ppermute(array, axis, [(i, i ^ bit) for i in range(lax.axis_size(axis))])


def summed_over_heads(attended, far, out_weight, count):
    def project(added, far_core, far_next, part, parts, out_type, name):
        return project_call(attended, out_weight, added, far_core, far_next, part, parts, count, out_type, name)

    *fars, near = rest_call(attended, out_weight, count)
    got_fars = [swapped(x, "head", 1) for x in (far, *fars)]
    sents = [project(got_fars[part], 0, 1, part, PARTS, jnp.bfloat16, "sent") for part in range(PARTS)]
    gots = [swapped(x, "head", 2) for x in sents]
    got_near = swapped(near, "head", 1)
    kepts = [project(got_near, 0, 0, part, PARTS, jnp.float32, "kept") for part in range(PARTS)]
    me = lax.axis_index("head")
    whole = None
    for part, (kept, got) in enumerate(zip(kepts, gots)):
        for b in range(2, count.bit_length() - 1):
            kept = kept + got.astype(jnp.float32)
            pairs = kept.reshape(kept.shape[0] // 2, 2, *kept.shape[1:])
            bit = (me >> b) & 1
            sent = lax.dynamic_index_in_dim(pairs, 1 - bit, 1, keepdims=False)
            kept = lax.dynamic_index_in_dim(pairs, bit, 1, keepdims=False)
            got = swapped(sent.astype(jnp.bfloat16), "head", 1 << b)
        whole = output_call(kept[0], got[0], part, whole)
    return whole


def on_device(queries, key_vectors, value_vectors, out_weight, offsets):
    devices = lax.axis_size("ctx")
    heads = lax.axis_size("head")
    rows = queries.shape[0]
    pair_steps = (min(REACH, devices // 2) + 1) // 2

    def moved_by(array, target):
        route = []
        for position in range(devices):
            for head in range(heads):
                p, x, h = target(position // 2, position % 2, head)
                route.append((position * heads + head, (2 * p + x) * heads + h))
        return lax.ppermute(array, ("ctx", "head"), route)

    def shifted(pair, step):
        last = devices // 2 - 1

        def target(p, x, h):
            return (p, x, h ^ 1) if p < step - 1 else (p + 1 if p < last else step - 1, x, h)

        return tuple(moved_by(m, target) for m in pair)

    def across(pair, step):
        return tuple(moved_by(m, lambda p, x, h: (p, x, h ^ 1) if p < step else (p, 1 - x, h)) for m in pair)

    def after(pair, state):
        first, state = lax.optimization_barrier((pair[0], state))
        return (first, pair[1]), state

    def finished(starts, q, pair, back, state, out_weight):
        totals, alphas, weights = last_scores_call(starts, q, pair[0], back, state)
        attended, product = finish_call(pair[1], weights, totals, alphas, state[2], out_weight, heads)
        return summed_over_heads(attended, product, out_weight, heads)

    def near(queries, key_vectors, value_vectors, out_weight, offsets):
        own = (key_vectors, value_vectors)
        moved = shifted(own, 1)
        beside = across(own, 0)
        starts, q, state = own_call(offsets, queries, key_vectors, value_vectors)
        moved, state = after(moved, state)
        crossed = across(moved, 1)
        state = attend_call(starts, q, [(*moved, lambda x: 2)], state)
        state = attend_call(starts, q, [(*beside, lambda x: 2 * x - 1)], state)
        return finished(starts, q, crossed, lambda x: 1 + 2 * x, state, out_weight)

    def reaching(queries, key_vectors, value_vectors, out_weight, offsets):
        moved = (key_vectors, value_vectors)
        beside = across(moved, 0)
        starts, q, state = own_call(offsets, queries, key_vectors, value_vectors)
        waiting = [(*beside, lambda x: 2 * x - 1)]
        for step in range(1, pair_steps + 1):
            moved, state = after(shifted(moved, step), state)
            waiting.insert(0, (*moved, lambda x, step=step: 2 * step))
            crossed = across(moved, step)
            if step < pair_steps:
                for piece in waiting:
                    state = attend_call(starts, q, [piece], state)
                waiting = [(*crossed, lambda x, step=step: 2 * step - 1 + 2 * x)]
        for piece in waiting:
            state = attend_call(starts, q, [piece], state)
        return finished(starts, q, crossed, lambda x: 2 * pair_steps - 1 + 2 * x, state, out_weight)

    given = (queries, key_vectors, value_vectors, out_weight, offsets)
    if pair_steps == 1:
        return near(*given)
    return lax.cond(reach_call(offsets, rows)[0] > 0, reaching, near, *given)


def solution(mesh):
    placed = (P("ctx", "head"), P("ctx", "head"), P("ctx", "head"), P("head", None), P())
    return jax.shard_map(
        on_device, mesh=mesh, in_specs=placed, out_specs=P("head", "ctx"), check_vma=False
    )
```

```python
import jax
import jax.numpy as jnp
from jax import lax
from jax.experimental import pallas as pl
from jax.experimental.pallas import tpu as pltpu
from jax.sharding import PartitionSpec as P

HEAD_DIM = 128
REACH = 15
LOG2E = 1.4426950408889634
masked_score = -1e30
PARTS = 2
VMEM_LIMIT = 20 * 1024 * 1024

vmem = pl.BlockSpec(memory_space=pltpu.VMEM)
smem = pl.BlockSpec(memory_space=pltpu.SMEM)
hbm = pl.BlockSpec(memory_space=pltpu.HBM)


def in_hbm(array):
    return pltpu.with_memory_space_constraint(array, pltpu.HBM)


def in_vmem(arrays):
    return [pltpu.with_memory_space_constraint(a, pltpu.VMEM) for a in arrays]


def params():
    return pltpu.CompilerParams(vmem_limit_bytes=VMEM_LIMIT)


def document_starts(offsets, first, rows):
    positions = first + lax.broadcasted_iota(jnp.int32, (1, rows), 1)
    starts = jnp.zeros((1, rows), jnp.int32)
    for i in range(1, offsets.shape[0] - 1):
        starts = jnp.where(positions >= offsets[i], offsets[i], starts)
    return starts


def scores_of(keys, query):
    return lax.dot_general(keys, query, (((1,), (1,)), ((), ())), preferred_element_type=jnp.float32)


def visible_keys(starts, key_start, rows, first):
    key_pos = key_start + lax.broadcasted_iota(jnp.int32, (rows, 1), 0)
    visible = key_pos >= starts
    if first is not None:
        visible = visible & (key_pos <= first + lax.broadcasted_iota(jnp.int32, (1, rows), 1))
    return visible


def score_block(q_ref, k_ref, visible, before):
    factor = HEAD_DIM ** -0.5 * LOG2E
    heads = q_ref.shape[1] // HEAD_DIM
    each = heads // (k_ref.shape[1] // HEAD_DIM)
    groups = [h // each for h in range(heads)]
    scores = [
        scores_of(k_ref[:, g * HEAD_DIM : (g + 1) * HEAD_DIM], q_ref[:, h * HEAD_DIM : (h + 1) * HEAD_DIM])
        for h, g in enumerate(groups)
    ]
    scores = [jnp.where(visible, s, masked_score) for s in scores]
    tops = [jnp.max(s, axis=0, keepdims=True) for s in scores]
    if before is not None:
        olds = [before[0][h : h + 1, :] for h in range(heads)]
        tops = [jnp.maximum(old, top) for old, top in zip(olds, tops)]
    weights = [jnp.exp2((s - top) * factor) for s, top in zip(scores, tops)]
    totals = [jnp.sum(w, axis=0, keepdims=True) for w in weights]
    weights = [w.astype(jnp.bfloat16) for w in weights]
    if before is None:
        return tops, totals, weights, None
    alphas = [jnp.exp2((old - top) * factor) for old, top in zip(olds, tops)]
    totals = [before[1][h : h + 1, :] * alphas[h] + totals[h] for h in range(heads)]
    return tops, totals, weights, alphas


def value_block(v_ref, weights, alphas, acc_ref):
    groups = v_ref.shape[1] // HEAD_DIM
    each = len(weights) // groups
    values = [v_ref[:, g * HEAD_DIM : (g + 1) * HEAD_DIM].T for g in range(groups)]
    sums = [jnp.dot(values[h // each], w, preferred_element_type=jnp.float32) for h, w in enumerate(weights)]
    if alphas is None:
        return sums
    return [acc_ref[h] * alphas[h] + s for h, s in enumerate(sums)]


def store_rows(ref, rows):
    for h, row in enumerate(rows):
        ref[h : h + 1, :] = row


def state_shapes(heads, rows):
    return [
        jax.ShapeDtypeStruct((heads, rows), jnp.float32),
        jax.ShapeDtypeStruct((heads, rows), jnp.float32),
        jax.ShapeDtypeStruct((heads, HEAD_DIM, rows), jnp.float32),
    ]


def first_row(rows):
    return lax.axis_index("ctx") * rows


def reach_call(offsets, rows):
    def kernel(offsets_ref, far_ref):
        far = jnp.int32(0)
        for i in range(offsets_ref.shape[0] - 1):
            steps = (offsets_ref[i + 1] - 1) // (2 * rows) - offsets_ref[i] // (2 * rows)
            far = jnp.maximum(far, jnp.where(steps >= 2, 1, 0))
        far_ref[0] = far

    return pl.pallas_call(
        kernel,
        out_shape=pltpu.SMEM((1,), jnp.int32),
        in_specs=[smem],
        out_specs=smem,
        name="reach",
    )(in_hbm(offsets))


def own_call(offsets, q, keys, values):
    rows, width = q.shape

    def kernel(offsets_in, q_in, k_in, v_in, starts_ref, q_ref, top_ref, total_ref, acc_ref, offsets_ref, k_ref, v_ref, sems):
        copies = [
            pltpu.make_async_copy(source, target, sems.at[i])
            for i, (source, target) in enumerate(((offsets_in, offsets_ref), (k_in, k_ref), (q_in, q_ref), (v_in, v_ref)))
        ]
        for copy in copies:
            copy.start()
        copies[0].wait()
        first = first_row(rows)
        starts = document_starts(offsets_ref, first, rows)
        starts_ref[...] = starts
        visible = visible_keys(starts, first, rows, first)
        for copy in copies[1:]:
            copy.wait()
        tops, totals, weights, _ = score_block(q_ref, k_ref, visible, None)
        store_rows(top_ref, tops)
        store_rows(total_ref, totals)
        for h, out in enumerate(value_block(v_ref, weights, None, None)):
            acc_ref[h] = out

    outs = pl.pallas_call(
        kernel,
        out_shape=[
            jax.ShapeDtypeStruct((1, rows), jnp.int32),
            jax.ShapeDtypeStruct(q.shape, q.dtype),
            *state_shapes(width // HEAD_DIM, rows),
        ],
        in_specs=[hbm] * 4,
        out_specs=[vmem] * 5,
        scratch_shapes=[
            pltpu.SMEM(offsets.shape, offsets.dtype),
            *[pltpu.VMEM(x.shape, x.dtype) for x in (keys, values)],
            pltpu.SemaphoreType.DMA((4,)),
        ],
        compiler_params=params(),
        cost_estimate=cost(width, rows, 1),
        name="own",
    )(*[in_hbm(x) for x in (offsets, q, keys, values)])
    return *outs[:2], outs[2:]


def cost(width, rows, blocks):
    return pl.CostEstimate(flops=20 * width * rows * rows * blocks, bytes_accessed=0, transcendentals=0)


def reached(back, rows):
    position = lax.axis_index("ctx")
    block = position - back(lax.rem(position, 2))
    return block * rows, (block >= 0) & (block <= position)


def attend_call(starts, q, keys, values, back, state):
    rows, width = q.shape

    def kernel(starts_ref, q_ref, k_ref, v_ref, *refs):
        before, after = refs[:3], refs[3:]
        key_start, seen = reached(back, rows)

        @pl.when(seen)
        def _():
            visible = visible_keys(starts_ref[...], key_start, rows, None)
            tops, totals, weights, alphas = score_block(q_ref, k_ref, visible, before)
            store_rows(after[0], tops)
            store_rows(after[1], totals)
            for h, out in enumerate(value_block(v_ref, weights, alphas, before[2])):
                after[2][h] = out

        @pl.when(jnp.logical_not(seen))
        def _():
            for old, new in zip(before, after):
                new[...] = old[...]

    return pl.pallas_call(
        kernel,
        out_shape=state_shapes(width // HEAD_DIM, rows),
        in_specs=[vmem] * 7,
        out_specs=[vmem] * 3,
        input_output_aliases={4 + i: i for i in range(3)},
        compiler_params=params(),
        cost_estimate=cost(width, rows, 1),
        name="attend",
    )(*in_vmem([starts, q, keys, values, *state]))


def last_scores_call(starts, q, keys, back, state):
    rows, width = q.shape
    heads = width // HEAD_DIM

    def kernel(starts_ref, q_ref, k_ref, top_ref, old_total_ref, total_ref, alpha_ref, weights_ref):
        key_start, seen = reached(back, rows)

        @pl.when(seen)
        def _():
            visible = visible_keys(starts_ref[...], key_start, rows, None)
            _, totals, weights, alphas = score_block(q_ref, k_ref, visible, (top_ref, old_total_ref))
            store_rows(total_ref, totals)
            store_rows(alpha_ref, alphas)
            for h, w in enumerate(weights):
                weights_ref[h] = w

        @pl.when(jnp.logical_not(seen))
        def _():
            total_ref[...] = old_total_ref[...]
            alpha_ref[...] = jnp.ones_like(alpha_ref)
            weights_ref[...] = jnp.zeros_like(weights_ref)

    return pl.pallas_call(
        kernel,
        out_shape=[
            jax.ShapeDtypeStruct((heads, rows), jnp.float32),
            jax.ShapeDtypeStruct((heads, rows), jnp.float32),
            jax.ShapeDtypeStruct((heads, rows, rows), jnp.bfloat16),
        ],
        in_specs=[vmem] * 5,
        out_specs=[vmem] * 3,
        compiler_params=params(),
        cost_estimate=cost(width, rows, 1),
        name="last_scores",
    )(*in_vmem([starts, q, keys, state[0], state[1]]))


def project_into(out_ref, att_ref, w_ref, added_ref, far_core, far_next, part, parts):
    size = out_ref.shape[2]
    block = size * parts
    added_start = 0 if added_ref is None or added_ref.shape[2] == size else part * size
    step = min(size, 256)
    me = lax.axis_index("head")
    bits = (me % 2 + far_core) % 2 + 2 * ((me // 2 + far_next) % 2)
    first = pl.multiple_of(bits * block, block)
    for i in range(out_ref.shape[0]):
        for start in range(0, size, step):
            cut = slice(start, start + step)
            columns = w_ref[:, pl.ds(first + 4 * i * block + part * size + start, step)]
            value = jnp.dot(att_ref[...], columns, preferred_element_type=jnp.float32)
            if added_ref is not None:
                value = value + added_ref[i, :, added_start + start : added_start + start + step].astype(jnp.float32)
            out_ref[i, :, cut] = value.astype(out_ref.dtype)


def by_first_exchange():
    return lax.rem(lax.axis_index("ctx") // 2, 2) == 1


def finish_call(values, weights, totals, alphas, acc, out_weight, count):
    heads, _, rows = acc.shape
    size = out_weight.shape[1] // count // PARTS

    n = len(values)

    def kernel(*refs):
        p_ref, total_ref, alpha_ref, acc_ref, w_ref, att_ref, far_ref = refs[n:]
        v = refs[0][...] if n == 1 else jnp.where(by_first_exchange(), refs[0][...], refs[1][...])
        scales = [alpha_ref[h : h + 1, :] for h in range(heads)]
        outs = value_block(v, [p_ref[h] for h in range(heads)], scales, acc_ref)
        for h, out in enumerate(outs):
            head = out * (1.0 / total_ref[h : h + 1, :])
            att_ref[:, h * HEAD_DIM : (h + 1) * HEAD_DIM] = head.T.astype(jnp.bfloat16)
        project_into(far_ref, att_ref, w_ref, None, 1, 1, 0, PARTS)

    return pl.pallas_call(
        kernel,
        out_shape=[
            jax.ShapeDtypeStruct((rows, heads * HEAD_DIM), jnp.bfloat16),
            jax.ShapeDtypeStruct((count // 4, rows, size), jnp.bfloat16),
        ],
        in_specs=[vmem] * (n + 5),
        out_specs=[vmem] * 2,
        compiler_params=params(),
        name="finish",
    )(*in_vmem([*values, weights, totals, alphas, acc]), out_weight)


def rest_call(attended, out_weight, count):
    rows, depth = attended.shape
    block = out_weight.shape[1] // count

    def kernel(att_ref, w_ref, *refs):
        for part in range(1, PARTS):
            project_into(refs[part - 1], att_ref, w_ref, None, 1, 1, part, PARTS)
        project_into(refs[-1], att_ref, w_ref, None, 1, 0, 0, 1)

    sizes = [block // PARTS] * (PARTS - 1) + [block]
    return pl.pallas_call(
        kernel,
        out_shape=[jax.ShapeDtypeStruct((count // 4, rows, size), jnp.bfloat16) for size in sizes],
        in_specs=[vmem] * 2,
        out_specs=[vmem] * PARTS,
        compiler_params=params(),
        cost_estimate=pl.CostEstimate(flops=2 * rows * depth * sum(sizes) * (count // 4), bytes_accessed=0, transcendentals=0),
        name="rest",
    )(*in_vmem([attended]), out_weight)


def project_call(attended, out_weight, added, far_core, far_next, part, parts, count, out_type, name):
    rows, depth = attended.shape
    size = out_weight.shape[1] // count // parts

    def kernel(att_ref, w_ref, *refs):
        project_into(refs[-1], att_ref, w_ref, refs[0] if len(refs) > 1 else None, far_core, far_next, part, parts)

    more = [] if added is None else [added]
    return pl.pallas_call(
        kernel,
        out_shape=jax.ShapeDtypeStruct((count // 4, rows, size), out_type),
        in_specs=[vmem] * (2 + len(more)),
        out_specs=vmem,
        compiler_params=params(),
        cost_estimate=pl.CostEstimate(flops=2 * rows * depth * size * (count // 4), bytes_accessed=0, transcendentals=0),
        name=name,
    )(*in_vmem([attended]), out_weight, *in_vmem(more))


def output_call(kept, arrived, part, whole):
    rows, size = kept.shape

    def kernel(kept_ref, arrived_ref, *refs):
        out_ref, held, sem = refs[-3:]
        held[...] = (kept_ref[...] + arrived_ref[...].astype(jnp.float32)).T.astype(jnp.bfloat16)
        copy = pltpu.make_async_copy(held, out_ref.at[part * size : (part + 1) * size], sem)
        copy.start()
        copy.wait()

    more = [] if whole is None else [in_hbm(whole)]
    return pl.pallas_call(
        kernel,
        out_shape=jax.ShapeDtypeStruct((size * PARTS, rows), jnp.bfloat16),
        in_specs=[vmem] * 2 + [hbm] * len(more),
        out_specs=hbm,
        scratch_shapes=[pltpu.VMEM((size, rows), jnp.bfloat16), pltpu.SemaphoreType.DMA],
        input_output_aliases={2: 0} if more else {},
        compiler_params=params(),
        name="output",
    )(*in_vmem([kept, arrived]), *more)


def swapped(array, axis, bit):
    return lax.ppermute(array, axis, [(i, i ^ bit) for i in range(lax.axis_size(axis))])


def summed_over_heads(attended, far, out_weight, count):
    def project(added, far_core, far_next, part, parts, out_type, name):
        return project_call(attended, out_weight, added, far_core, far_next, part, parts, count, out_type, name)

    *fars, near = rest_call(attended, out_weight, count)
    got_fars = [swapped(x, "head", 1) for x in (far, *fars)]
    sents = [project(got_fars[part], 0, 1, part, PARTS, jnp.bfloat16, "sent") for part in range(PARTS)]
    gots = [swapped(x, "head", 2) for x in sents]
    got_near = swapped(near, "head", 1)
    kepts = [project(got_near, 0, 0, part, PARTS, jnp.float32, "kept") for part in range(PARTS)]
    me = lax.axis_index("head")
    whole = None
    for part, (kept, got) in enumerate(zip(kepts, gots)):
        for b in range(2, count.bit_length() - 1):
            kept = kept + got.astype(jnp.float32)
            pairs = kept.reshape(kept.shape[0] // 2, 2, *kept.shape[1:])
            bit = (me >> b) & 1
            sent = lax.dynamic_index_in_dim(pairs, 1 - bit, 1, keepdims=False)
            kept = lax.dynamic_index_in_dim(pairs, bit, 1, keepdims=False)
            got = swapped(sent.astype(jnp.bfloat16), "head", 1 << b)
        whole = output_call(kept[0], got[0], part, whole)
    return whole


def on_device(queries, key_vectors, value_vectors, out_weight, offsets):
    devices = lax.axis_size("ctx")
    heads = lax.axis_size("head")
    rows = queries.shape[0]
    pair_steps = (min(REACH, devices // 2) + 1) // 2

    def moved_by(array, target):
        route = []
        for position in range(devices):
            for head in range(heads):
                p, x, h = target(position // 2, position % 2, head)
                route.append((position * heads + head, (2 * p + x) * heads + h))
        return lax.ppermute(array, ("ctx", "head"), route)

    def shifted(pair, step):
        last = devices // 2 - 1

        def target(p, x, h):
            return (p, x, h ^ 1) if p < step - 1 else (p + 1 if p < last else step - 1, x, h)

        return tuple(moved_by(m, target) for m in pair)

    def across(pair, step):
        return tuple(moved_by(m, lambda p, x, h: (p, x, h ^ 1) if p < step else (p, 1 - x, h)) for m in pair)

    def exchanged(array):
        pairs = devices // 2

        def target(shift, p, x, h):
            other = ((p + shift) ^ 1) - shift
            return (other, x, h) if 0 <= other < pairs else (p, x, h ^ 1)

        return tuple(moved_by(array, lambda p, x, h, shift=shift: target(shift, p, x, h)) for shift in (0, 1))

    def after(pair, state):
        first, state = lax.optimization_barrier((pair[0], state))
        return (first, pair[1]), state

    def finished(starts, q, pair, back, state, out_weight):
        totals, alphas, weights = last_scores_call(starts, q, pair[0], back, state)
        attended, product = finish_call(pair[1:], weights, totals, alphas, state[2], out_weight, heads)
        return summed_over_heads(attended, product, out_weight, heads)

    def near(queries, key_vectors, value_vectors, out_weight, offsets):
        own = (key_vectors, value_vectors)
        moved = shifted(own, 1)
        beside = across(own, 0)
        starts, q, state = own_call(offsets, queries, key_vectors, value_vectors)
        moved, state = after(moved, state)
        crossed = across(moved[:1], 1) + exchanged(beside[1])
        state = attend_call(starts, q, *moved, lambda x: 2, state)
        state = attend_call(starts, q, *beside, lambda x: 2 * x - 1, state)
        return finished(starts, q, crossed, lambda x: 1 + 2 * x, state, out_weight)

    def reaching(queries, key_vectors, value_vectors, out_weight, offsets):
        moved = (key_vectors, value_vectors)
        beside = across(moved, 0)
        starts, q, state = own_call(offsets, queries, key_vectors, value_vectors)
        waiting = [(*beside, lambda x: 2 * x - 1)]
        for step in range(1, pair_steps + 1):
            moved, state = after(shifted(moved, step), state)
            waiting.insert(0, (*moved, lambda x, step=step: 2 * step))
            crossed = across(moved, step)
            if step < pair_steps:
                for piece in waiting:
                    state = attend_call(starts, q, *piece, state)
                waiting = [(*crossed, lambda x, step=step: 2 * step - 1 + 2 * x)]
        for piece in waiting:
            state = attend_call(starts, q, *piece, state)
        return finished(starts, q, crossed, lambda x: 2 * pair_steps - 1 + 2 * x, state, out_weight)

    given = (queries, key_vectors, value_vectors, out_weight, offsets)
    if pair_steps == 1:
        return near(*given)
    return lax.cond(reach_call(offsets, rows)[0] > 0, reaching, near, *given)


def solution(mesh):
    placed = (P("ctx", "head"), P("ctx", "head"), P("ctx", "head"), P("head", None), P())
    return jax.shard_map(
        on_device, mesh=mesh, in_specs=placed, out_specs=P("head", "ctx"), check_vma=False
    )
```

```python
import jax
import jax.numpy as jnp
from jax import lax
from jax.experimental import pallas as pl
from jax.experimental.pallas import tpu as pltpu
from jax.sharding import PartitionSpec as P

HEAD_DIM = 128
REACH = 15
LOG2E = 1.4426950408889634
masked_score = -1e30
PARTS = 2
VMEM_LIMIT = 20 * 1024 * 1024

vmem = pl.BlockSpec(memory_space=pltpu.VMEM)
smem = pl.BlockSpec(memory_space=pltpu.SMEM)
hbm = pl.BlockSpec(memory_space=pltpu.HBM)


def in_hbm(array):
    return pltpu.with_memory_space_constraint(array, pltpu.HBM)


def in_vmem(arrays):
    return [pltpu.with_memory_space_constraint(a, pltpu.VMEM) for a in arrays]


def params():
    return pltpu.CompilerParams(vmem_limit_bytes=VMEM_LIMIT)


def document_starts(offsets, first, rows):
    positions = first + lax.broadcasted_iota(jnp.int32, (1, rows), 1)
    starts = jnp.zeros((1, rows), jnp.int32)
    for i in range(1, offsets.shape[0] - 1):
        starts = jnp.where(positions >= offsets[i], offsets[i], starts)
    return starts


def scores_of(keys, query):
    return lax.dot_general(keys, query, (((1,), (1,)), ((), ())), preferred_element_type=jnp.float32)


def visible_keys(starts, key_start, rows, first):
    key_pos = key_start + lax.broadcasted_iota(jnp.int32, (rows, 1), 0)
    visible = key_pos >= starts
    if first is not None:
        visible = visible & (key_pos <= first + lax.broadcasted_iota(jnp.int32, (1, rows), 1))
    return visible


def score_block(q_ref, k_ref, visible, before):
    factor = HEAD_DIM ** -0.5 * LOG2E
    heads = q_ref.shape[1] // HEAD_DIM
    each = heads // (k_ref.shape[1] // HEAD_DIM)
    groups = [h // each for h in range(heads)]
    scores = [
        scores_of(k_ref[:, g * HEAD_DIM : (g + 1) * HEAD_DIM], q_ref[:, h * HEAD_DIM : (h + 1) * HEAD_DIM])
        for h, g in enumerate(groups)
    ]
    scores = [jnp.where(visible, s, masked_score) for s in scores]
    tops = [jnp.max(s, axis=0, keepdims=True) for s in scores]
    if before is not None:
        olds = [before[0][h : h + 1, :] for h in range(heads)]
        tops = [jnp.maximum(old, top) for old, top in zip(olds, tops)]
    weights = [jnp.exp2((s - top) * factor) for s, top in zip(scores, tops)]
    totals = [jnp.sum(w, axis=0, keepdims=True) for w in weights]
    weights = [w.astype(jnp.bfloat16) for w in weights]
    if before is None:
        return tops, totals, weights, None
    alphas = [jnp.exp2((old - top) * factor) for old, top in zip(olds, tops)]
    totals = [before[1][h : h + 1, :] * alphas[h] + totals[h] for h in range(heads)]
    return tops, totals, weights, alphas


def value_block(v_ref, weights, alphas, acc_ref):
    groups = v_ref.shape[1] // HEAD_DIM
    each = len(weights) // groups
    values = [v_ref[:, g * HEAD_DIM : (g + 1) * HEAD_DIM].T for g in range(groups)]
    sums = [jnp.dot(values[h // each], w, preferred_element_type=jnp.float32) for h, w in enumerate(weights)]
    if alphas is None:
        return sums
    return [acc_ref[h] * alphas[h] + s for h, s in enumerate(sums)]


def store_rows(ref, rows):
    for h, row in enumerate(rows):
        ref[h : h + 1, :] = row


def state_shapes(heads, rows):
    return [
        jax.ShapeDtypeStruct((heads, rows), jnp.float32),
        jax.ShapeDtypeStruct((heads, rows), jnp.float32),
        jax.ShapeDtypeStruct((heads, HEAD_DIM, rows), jnp.float32),
    ]


def first_row(rows):
    return lax.axis_index("ctx") * rows


def reach_call(offsets, rows):
    def kernel(offsets_ref, far_ref):
        far = jnp.int32(0)
        for i in range(offsets_ref.shape[0] - 1):
            steps = (offsets_ref[i + 1] - 1) // (2 * rows) - offsets_ref[i] // (2 * rows)
            far = jnp.maximum(far, jnp.where(steps >= 2, 1, 0))
        far_ref[0] = far

    return pl.pallas_call(
        kernel,
        out_shape=pltpu.SMEM((1,), jnp.int32),
        in_specs=[smem],
        out_specs=smem,
        name="reach",
    )(in_hbm(offsets))


def own_call(offsets, q, keys, values):
    rows, width = q.shape

    def kernel(offsets_in, q_in, k_in, v_in, starts_ref, q_ref, top_ref, total_ref, acc_ref, offsets_ref, k_ref, v_ref, sems):
        copies = [
            pltpu.make_async_copy(source, target, sems.at[i])
            for i, (source, target) in enumerate(((offsets_in, offsets_ref), (k_in, k_ref), (q_in, q_ref), (v_in, v_ref)))
        ]
        for copy in copies:
            copy.start()
        copies[0].wait()
        first = first_row(rows)
        starts = document_starts(offsets_ref, first, rows)
        starts_ref[...] = starts
        visible = visible_keys(starts, first, rows, first)
        for copy in copies[1:]:
            copy.wait()
        tops, totals, weights, _ = score_block(q_ref, k_ref, visible, None)
        store_rows(top_ref, tops)
        store_rows(total_ref, totals)
        for h, out in enumerate(value_block(v_ref, weights, None, None)):
            acc_ref[h] = out

    outs = pl.pallas_call(
        kernel,
        out_shape=[
            jax.ShapeDtypeStruct((1, rows), jnp.int32),
            jax.ShapeDtypeStruct(q.shape, q.dtype),
            *state_shapes(width // HEAD_DIM, rows),
        ],
        in_specs=[hbm] * 4,
        out_specs=[vmem] * 5,
        scratch_shapes=[
            pltpu.SMEM(offsets.shape, offsets.dtype),
            *[pltpu.VMEM(x.shape, x.dtype) for x in (keys, values)],
            pltpu.SemaphoreType.DMA((4,)),
        ],
        compiler_params=params(),
        cost_estimate=cost(width, rows, 1),
        name="own",
    )(*[in_hbm(x) for x in (offsets, q, keys, values)])
    return *outs[:2], outs[2:]


def cost(width, rows, blocks):
    return pl.CostEstimate(flops=20 * width * rows * rows * blocks, bytes_accessed=0, transcendentals=0)


def reached(back, rows):
    position = lax.axis_index("ctx")
    block = position - back(lax.rem(position, 2))
    return block * rows, (block >= 0) & (block <= position)


def attend_call(starts, q, keys, values, back, state):
    rows, width = q.shape

    def kernel(starts_ref, q_ref, k_ref, v_ref, *refs):
        before, after = refs[:3], refs[3:]
        key_start, seen = reached(back, rows)

        @pl.when(seen)
        def _():
            visible = visible_keys(starts_ref[...], key_start, rows, None)
            tops, totals, weights, alphas = score_block(q_ref, k_ref, visible, before)
            store_rows(after[0], tops)
            store_rows(after[1], totals)
            for h, out in enumerate(value_block(v_ref, weights, alphas, before[2])):
                after[2][h] = out

        @pl.when(jnp.logical_not(seen))
        def _():
            for old, new in zip(before, after):
                new[...] = old[...]

    return pl.pallas_call(
        kernel,
        out_shape=state_shapes(width // HEAD_DIM, rows),
        in_specs=[vmem] * 7,
        out_specs=[vmem] * 3,
        input_output_aliases={4 + i: i for i in range(3)},
        compiler_params=params(),
        cost_estimate=cost(width, rows, 1),
        name="attend",
    )(*in_vmem([starts, q, keys, values, *state]))


def last_scores_call(starts, q, keys, back, state):
    rows, width = q.shape
    heads = width // HEAD_DIM

    def kernel(starts_ref, q_ref, k_ref, top_ref, old_total_ref, total_ref, alpha_ref, weights_ref):
        key_start, seen = reached(back, rows)

        @pl.when(seen)
        def _():
            visible = visible_keys(starts_ref[...], key_start, rows, None)
            _, totals, weights, alphas = score_block(q_ref, k_ref, visible, (top_ref, old_total_ref))
            store_rows(total_ref, totals)
            store_rows(alpha_ref, alphas)
            for h, w in enumerate(weights):
                weights_ref[h] = w

        @pl.when(jnp.logical_not(seen))
        def _():
            total_ref[...] = old_total_ref[...]
            alpha_ref[...] = jnp.ones_like(alpha_ref)
            weights_ref[...] = jnp.zeros_like(weights_ref)

    return pl.pallas_call(
        kernel,
        out_shape=[
            jax.ShapeDtypeStruct((heads, rows), jnp.float32),
            jax.ShapeDtypeStruct((heads, rows), jnp.float32),
            jax.ShapeDtypeStruct((heads, rows, rows), jnp.bfloat16),
        ],
        in_specs=[vmem] * 5,
        out_specs=[vmem] * 3,
        compiler_params=params(),
        cost_estimate=cost(width, rows, 1),
        name="last_scores",
    )(*in_vmem([starts, q, keys, state[0], state[1]]))


def project_into(out_ref, att_ref, w_ref, added_ref, far_core, far_next, part, parts):
    size = out_ref.shape[2]
    block = size * parts
    added_start = 0 if added_ref is None or added_ref.shape[2] == size else part * size
    step = min(size, 256)
    me = lax.axis_index("head")
    bits = (me % 2 + far_core) % 2 + 2 * ((me // 2 + far_next) % 2)
    first = pl.multiple_of(bits * block, block)
    for i in range(out_ref.shape[0]):
        for start in range(0, size, step):
            cut = slice(start, start + step)
            columns = w_ref[:, pl.ds(first + 4 * i * block + part * size + start, step)]
            value = jnp.dot(att_ref[...], columns, preferred_element_type=jnp.float32)
            if added_ref is not None:
                value = value + added_ref[i, :, added_start + start : added_start + start + step].astype(jnp.float32)
            out_ref[i, :, cut] = value.astype(out_ref.dtype)


def by_first_exchange():
    return lax.rem(lax.axis_index("ctx") // 2, 2) == 1


def finish_call(values, weights, totals, alphas, acc, out_weight, count):
    heads, _, rows = acc.shape
    size = out_weight.shape[1] // count // PARTS

    n = len(values)

    def kernel(*refs):
        p_ref, total_ref, alpha_ref, acc_ref, w_ref, att_ref, far_ref = refs[n:]
        v = refs[0][...] if n == 1 else jnp.where(by_first_exchange(), refs[0][...], refs[1][...])
        scales = [alpha_ref[h : h + 1, :] for h in range(heads)]
        outs = value_block(v, [p_ref[h] for h in range(heads)], scales, acc_ref)
        for h, out in enumerate(outs):
            head = out * (1.0 / total_ref[h : h + 1, :])
            att_ref[:, h * HEAD_DIM : (h + 1) * HEAD_DIM] = head.T.astype(jnp.bfloat16)
        project_into(far_ref, att_ref, w_ref, None, 1, 1, 0, PARTS)

    return pl.pallas_call(
        kernel,
        out_shape=[
            jax.ShapeDtypeStruct((rows, heads * HEAD_DIM), jnp.bfloat16),
            jax.ShapeDtypeStruct((count // 4, rows, size), jnp.bfloat16),
        ],
        in_specs=[vmem] * (n + 5),
        out_specs=[vmem] * 2,
        compiler_params=params(),
        name="finish",
    )(*in_vmem([*values, weights, totals, alphas, acc]), out_weight)


def rest_call(attended, out_weight, count):
    rows, depth = attended.shape
    block = out_weight.shape[1] // count

    def kernel(att_ref, w_ref, *refs):
        for part in range(1, PARTS):
            project_into(refs[part - 1], att_ref, w_ref, None, 1, 1, part, PARTS)
        project_into(refs[-1], att_ref, w_ref, None, 1, 0, 0, 1)

    sizes = [block // PARTS] * (PARTS - 1) + [block]
    return pl.pallas_call(
        kernel,
        out_shape=[jax.ShapeDtypeStruct((count // 4, rows, size), jnp.bfloat16) for size in sizes],
        in_specs=[vmem] * 2,
        out_specs=[vmem] * PARTS,
        compiler_params=params(),
        cost_estimate=pl.CostEstimate(flops=2 * rows * depth * sum(sizes) * (count // 4), bytes_accessed=0, transcendentals=0),
        name="rest",
    )(*in_vmem([attended]), out_weight)


def project_call(attended, out_weight, added, far_core, far_next, part, parts, count, out_type, name):
    rows, depth = attended.shape
    size = out_weight.shape[1] // count // parts

    def kernel(att_ref, w_ref, *refs):
        project_into(refs[-1], att_ref, w_ref, refs[0] if len(refs) > 1 else None, far_core, far_next, part, parts)

    more = [] if added is None else [added]
    return pl.pallas_call(
        kernel,
        out_shape=jax.ShapeDtypeStruct((count // 4, rows, size), out_type),
        in_specs=[vmem] * (2 + len(more)),
        out_specs=vmem,
        compiler_params=params(),
        cost_estimate=pl.CostEstimate(flops=2 * rows * depth * size * (count // 4), bytes_accessed=0, transcendentals=0),
        name=name,
    )(*in_vmem([attended]), out_weight, *in_vmem(more))


def output_call(kept, arrived, part, whole):
    rows, size = kept.shape

    def kernel(kept_ref, arrived_ref, *refs):
        out_ref, held, sem = refs[-3:]
        held[...] = (kept_ref[...] + arrived_ref[...].astype(jnp.float32)).T.astype(jnp.bfloat16)
        copy = pltpu.make_async_copy(held, out_ref.at[part * size : (part + 1) * size], sem)
        copy.start()
        copy.wait()

    more = [] if whole is None else [in_hbm(whole)]
    return pl.pallas_call(
        kernel,
        out_shape=jax.ShapeDtypeStruct((size * PARTS, rows), jnp.bfloat16),
        in_specs=[vmem] * 2 + [hbm] * len(more),
        out_specs=hbm,
        scratch_shapes=[pltpu.VMEM((size, rows), jnp.bfloat16), pltpu.SemaphoreType.DMA],
        input_output_aliases={2: 0} if more else {},
        compiler_params=params(),
        name="output",
    )(*in_vmem([kept, arrived]), *more)


def swapped(array, axis, bit):
    return lax.ppermute(array, axis, [(i, i ^ bit) for i in range(lax.axis_size(axis))])


def summed_over_heads(attended, far, out_weight, count):
    def project(added, far_core, far_next, part, parts, out_type, name):
        return project_call(attended, out_weight, added, far_core, far_next, part, parts, count, out_type, name)

    *fars, near = rest_call(attended, out_weight, count)
    got_fars = [swapped(x, "head", 1) for x in (far, *fars)]
    sents = [project(got_fars[part], 0, 1, part, PARTS, jnp.bfloat16, "sent") for part in range(PARTS)]
    gots = [swapped(x, "head", 2) for x in sents]
    got_near = swapped(near, "head", 1)
    kepts = [project(got_near, 0, 0, part, PARTS, jnp.float32, "kept") for part in range(PARTS)]
    me = lax.axis_index("head")
    whole = None
    for part, (kept, got) in enumerate(zip(kepts, gots)):
        for b in range(2, count.bit_length() - 1):
            kept = kept + got.astype(jnp.float32)
            pairs = kept.reshape(kept.shape[0] // 2, 2, *kept.shape[1:])
            bit = (me >> b) & 1
            sent = lax.dynamic_index_in_dim(pairs, 1 - bit, 1, keepdims=False)
            kept = lax.dynamic_index_in_dim(pairs, bit, 1, keepdims=False)
            got = swapped(sent.astype(jnp.bfloat16), "head", 1 << b)
        whole = output_call(kept[0], got[0], part, whole)
    return whole


def on_device(queries, key_vectors, value_vectors, out_weight, offsets):
    devices = lax.axis_size("ctx")
    heads = lax.axis_size("head")
    rows = queries.shape[0]
    pair_steps = (min(REACH, devices // 2) + 1) // 2

    def moved_by(array, target):
        route = []
        for position in range(devices):
            for head in range(heads):
                p, x, h = target(position // 2, position % 2, head)
                route.append((position * heads + head, (2 * p + x) * heads + h))
        return lax.ppermute(array, ("ctx", "head"), route)

    def shifted(pair, step):
        last = devices // 2 - 1

        def target(p, x, h):
            return (p, x, h ^ 1) if p < step - 1 else (p + 1 if p < last else step - 1, x, h)

        return tuple(moved_by(m, target) for m in pair)

    def across(pair, step):
        return tuple(moved_by(m, lambda p, x, h: (p, x, h ^ 1) if p < step else (p, 1 - x, h)) for m in pair)

    def exchanged(array):
        pairs = devices // 2

        def target(shift, p, x, h):
            other = ((p + shift) ^ 1) - shift
            return (other, x, h) if 0 <= other < pairs else (p, x, h ^ 1)

        return tuple(moved_by(array, lambda p, x, h, shift=shift: target(shift, p, x, h)) for shift in (0, 1))

    def after(pair, state):
        first, state = lax.optimization_barrier((pair[0], state))
        return (first, pair[1]), state

    def finished(starts, q, pair, back, state, out_weight):
        totals, alphas, weights = last_scores_call(starts, q, pair[0], back, state)
        attended, product = finish_call(pair[1:], weights, totals, alphas, state[2], out_weight, heads)
        return summed_over_heads(attended, product, out_weight, heads)

    def near(queries, key_vectors, value_vectors, out_weight, offsets):
        own = (key_vectors, value_vectors)
        moved = shifted(own, 1)
        beside = across(own, 0)
        starts, q, state = own_call(offsets, queries, key_vectors, value_vectors)
        moved, state = after(moved, state)
        crossed = across(moved[:1], 1) + exchanged(beside[1])
        state = attend_call(starts, q, *moved, lambda x: 2, state)
        state = attend_call(starts, q, *beside, lambda x: 2 * x - 1, state)
        return finished(starts, q, crossed, lambda x: 1 + 2 * x, state, out_weight)

    def reaching(queries, key_vectors, value_vectors, out_weight, offsets):
        moved = (key_vectors, value_vectors)
        beside = across(moved, 0)
        starts, q, state = own_call(offsets, queries, key_vectors, value_vectors)
        waiting = [(*beside, lambda x: 2 * x - 1)]
        for step in range(1, pair_steps + 1):
            moved, state = after(shifted(moved, step), state)
            waiting.insert(0 if step == 1 else 1, (*moved, lambda x, step=step: 2 * step))
            crossed = across(moved, step)
            if step < pair_steps:
                for piece in waiting:
                    state = attend_call(starts, q, *piece, state)
                waiting = [(*crossed, lambda x, step=step: 2 * step - 1 + 2 * x)]
        for piece in waiting:
            state = attend_call(starts, q, *piece, state)
        return finished(starts, q, crossed, lambda x: 2 * pair_steps - 1 + 2 * x, state, out_weight)

    given = (queries, key_vectors, value_vectors, out_weight, offsets)
    if pair_steps == 1:
        return near(*given)
    return lax.cond(reach_call(offsets, rows)[0] > 0, reaching, near, *given)


def solution(mesh):
    placed = (P("ctx", "head"), P("ctx", "head"), P("ctx", "head"), P("head", None), P())
    return jax.shard_map(
        on_device, mesh=mesh, in_specs=placed, out_specs=P("head", "ctx"), check_vma=False
    )
```

```python
import jax
import jax.numpy as jnp
from jax import lax
from jax.experimental import pallas as pl
from jax.experimental.pallas import tpu as pltpu
from jax.sharding import PartitionSpec as P

HEAD_DIM = 128
REACH = 15
LOG2E = 1.4426950408889634
masked_score = -1e30
PARTS = 2
VMEM_LIMIT = 20 * 1024 * 1024

vmem = pl.BlockSpec(memory_space=pltpu.VMEM)
smem = pl.BlockSpec(memory_space=pltpu.SMEM)
hbm = pl.BlockSpec(memory_space=pltpu.HBM)


def in_hbm(array):
    return pltpu.with_memory_space_constraint(array, pltpu.HBM)


def in_vmem(arrays):
    return [pltpu.with_memory_space_constraint(a, pltpu.VMEM) for a in arrays]


def params():
    return pltpu.CompilerParams(vmem_limit_bytes=VMEM_LIMIT)


def document_starts(offsets, first, rows):
    positions = first + lax.broadcasted_iota(jnp.int32, (1, rows), 1)
    starts = jnp.zeros((1, rows), jnp.int32)
    for i in range(1, offsets.shape[0] - 1):
        starts = jnp.where(positions >= offsets[i], offsets[i], starts)
    return starts


def scores_of(keys, query):
    return lax.dot_general(keys, query, (((1,), (1,)), ((), ())), preferred_element_type=jnp.float32)


def visible_keys(starts, key_start, rows, first):
    key_pos = key_start + lax.broadcasted_iota(jnp.int32, (rows, 1), 0)
    visible = key_pos >= starts
    if first is not None:
        visible = visible & (key_pos <= first + lax.broadcasted_iota(jnp.int32, (1, rows), 1))
    return visible


def score_block(q_ref, k_ref, visible, before):
    factor = HEAD_DIM ** -0.5 * LOG2E
    heads = q_ref.shape[1] // HEAD_DIM
    each = heads // (k_ref.shape[1] // HEAD_DIM)
    groups = [h // each for h in range(heads)]
    scores = [
        scores_of(k_ref[:, g * HEAD_DIM : (g + 1) * HEAD_DIM], q_ref[:, h * HEAD_DIM : (h + 1) * HEAD_DIM])
        for h, g in enumerate(groups)
    ]
    scores = [jnp.where(visible, s, masked_score) for s in scores]
    tops = [jnp.max(s, axis=0, keepdims=True) for s in scores]
    if before is not None:
        olds = [before[0][h : h + 1, :] for h in range(heads)]
        tops = [jnp.maximum(old, top) for old, top in zip(olds, tops)]
    weights = [jnp.exp2((s - top) * factor) for s, top in zip(scores, tops)]
    totals = [jnp.sum(w, axis=0, keepdims=True) for w in weights]
    weights = [w.astype(jnp.bfloat16) for w in weights]
    if before is None:
        return tops, totals, weights, None
    alphas = [jnp.exp2((old - top) * factor) for old, top in zip(olds, tops)]
    totals = [before[1][h : h + 1, :] * alphas[h] + totals[h] for h in range(heads)]
    return tops, totals, weights, alphas


def value_block(v_ref, weights, alphas, acc_ref):
    groups = v_ref.shape[1] // HEAD_DIM
    each = len(weights) // groups
    values = [v_ref[:, g * HEAD_DIM : (g + 1) * HEAD_DIM].T for g in range(groups)]
    sums = [jnp.dot(values[h // each], w, preferred_element_type=jnp.float32) for h, w in enumerate(weights)]
    if alphas is None:
        return sums
    return [acc_ref[h] * alphas[h] + s for h, s in enumerate(sums)]


def store_rows(ref, rows):
    for h, row in enumerate(rows):
        ref[h : h + 1, :] = row


def state_shapes(heads, rows):
    return [
        jax.ShapeDtypeStruct((heads, rows), jnp.float32),
        jax.ShapeDtypeStruct((heads, rows), jnp.float32),
        jax.ShapeDtypeStruct((heads, HEAD_DIM, rows), jnp.float32),
    ]


def first_row(rows):
    return lax.axis_index("ctx") * rows


def reach_call(offsets, rows):
    def kernel(offsets_ref, far_ref):
        far = jnp.int32(0)
        for i in range(offsets_ref.shape[0] - 1):
            steps = (offsets_ref[i + 1] - 1) // (2 * rows) - offsets_ref[i] // (2 * rows)
            far = jnp.maximum(far, jnp.where(steps >= 2, 1, 0))
        far_ref[0] = far

    return pl.pallas_call(
        kernel,
        out_shape=pltpu.SMEM((1,), jnp.int32),
        in_specs=[smem],
        out_specs=smem,
        name="reach",
    )(in_hbm(offsets))


def own_call(offsets, q, keys, values):
    rows, width = q.shape

    def kernel(offsets_in, q_in, k_in, v_in, starts_ref, q_ref, top_ref, total_ref, acc_ref, offsets_ref, k_ref, v_ref, sems):
        copies = [
            pltpu.make_async_copy(source, target, sems.at[i])
            for i, (source, target) in enumerate(((offsets_in, offsets_ref), (k_in, k_ref), (q_in, q_ref), (v_in, v_ref)))
        ]
        for copy in copies:
            copy.start()
        copies[0].wait()
        first = first_row(rows)
        starts = document_starts(offsets_ref, first, rows)
        starts_ref[...] = starts
        visible = visible_keys(starts, first, rows, first)
        for copy in copies[1:]:
            copy.wait()
        tops, totals, weights, _ = score_block(q_ref, k_ref, visible, None)
        store_rows(top_ref, tops)
        store_rows(total_ref, totals)
        for h, out in enumerate(value_block(v_ref, weights, None, None)):
            acc_ref[h] = out

    outs = pl.pallas_call(
        kernel,
        out_shape=[
            jax.ShapeDtypeStruct((1, rows), jnp.int32),
            jax.ShapeDtypeStruct(q.shape, q.dtype),
            *state_shapes(width // HEAD_DIM, rows),
        ],
        in_specs=[hbm] * 4,
        out_specs=[vmem] * 5,
        scratch_shapes=[
            pltpu.SMEM(offsets.shape, offsets.dtype),
            *[pltpu.VMEM(x.shape, x.dtype) for x in (keys, values)],
            pltpu.SemaphoreType.DMA((4,)),
        ],
        compiler_params=params(),
        cost_estimate=cost(width, rows, 1),
        name="own",
    )(*[in_hbm(x) for x in (offsets, q, keys, values)])
    return *outs[:2], outs[2:]


def cost(width, rows, blocks):
    return pl.CostEstimate(flops=20 * width * rows * rows * blocks, bytes_accessed=0, transcendentals=0)


def reached(back, rows):
    position = lax.axis_index("ctx")
    block = position - back(lax.rem(position, 2))
    return block * rows, (block >= 0) & (block <= position)


def attend_call(starts, q, keys, values, back, state):
    rows, width = q.shape

    def kernel(starts_ref, q_ref, k_ref, v_ref, *refs):
        before, after = refs[:3], refs[3:]
        key_start, seen = reached(back, rows)

        @pl.when(seen)
        def _():
            visible = visible_keys(starts_ref[...], key_start, rows, None)
            tops, totals, weights, alphas = score_block(q_ref, k_ref, visible, before)
            store_rows(after[0], tops)
            store_rows(after[1], totals)
            for h, out in enumerate(value_block(v_ref, weights, alphas, before[2])):
                after[2][h] = out

        @pl.when(jnp.logical_not(seen))
        def _():
            for old, new in zip(before, after):
                new[...] = old[...]

    return pl.pallas_call(
        kernel,
        out_shape=state_shapes(width // HEAD_DIM, rows),
        in_specs=[vmem] * 7,
        out_specs=[vmem] * 3,
        input_output_aliases={4 + i: i for i in range(3)},
        compiler_params=params(),
        cost_estimate=cost(width, rows, 1),
        name="attend",
    )(*in_vmem([starts, q, keys, values, *state]))


def last_scores_call(starts, q, keys, back, state):
    rows, width = q.shape
    heads = width // HEAD_DIM

    def kernel(starts_ref, q_ref, k_ref, top_ref, old_total_ref, total_ref, alpha_ref, weights_ref):
        key_start, seen = reached(back, rows)

        @pl.when(seen)
        def _():
            visible = visible_keys(starts_ref[...], key_start, rows, None)
            _, totals, weights, alphas = score_block(q_ref, k_ref, visible, (top_ref, old_total_ref))
            store_rows(total_ref, totals)
            store_rows(alpha_ref, alphas)
            for h, w in enumerate(weights):
                weights_ref[h] = w

        @pl.when(jnp.logical_not(seen))
        def _():
            total_ref[...] = old_total_ref[...]
            alpha_ref[...] = jnp.ones_like(alpha_ref)
            weights_ref[...] = jnp.zeros_like(weights_ref)

    return pl.pallas_call(
        kernel,
        out_shape=[
            jax.ShapeDtypeStruct((heads, rows), jnp.float32),
            jax.ShapeDtypeStruct((heads, rows), jnp.float32),
            jax.ShapeDtypeStruct((heads, rows, rows), jnp.bfloat16),
        ],
        in_specs=[vmem] * 5,
        out_specs=[vmem] * 3,
        compiler_params=params(),
        cost_estimate=cost(width, rows, 1),
        name="last_scores",
    )(*in_vmem([starts, q, keys, state[0], state[1]]))


def project_into(out_ref, att_ref, w_ref, added_ref, far_core, far_next, part, parts):
    size = out_ref.shape[2]
    block = size * parts
    added_start = 0 if added_ref is None or added_ref.shape[2] == size else part * size
    step = min(size, 256)
    me = lax.axis_index("head")
    bits = (me % 2 + far_core) % 2 + 2 * ((me // 2 + far_next) % 2)
    first = pl.multiple_of(bits * block, block)
    for i in range(out_ref.shape[0]):
        for start in range(0, size, step):
            cut = slice(start, start + step)
            columns = w_ref[:, pl.ds(first + 4 * i * block + part * size + start, step)]
            value = jnp.dot(att_ref[...], columns, preferred_element_type=jnp.float32)
            if added_ref is not None:
                value = value + added_ref[i, :, added_start + start : added_start + start + step].astype(jnp.float32)
            out_ref[i, :, cut] = value.astype(out_ref.dtype)


def by_first_exchange():
    return lax.rem(lax.axis_index("ctx") // 2, 2) == 1


def finish_call(values, weights, totals, alphas, acc, out_weight, count):
    heads, _, rows = acc.shape
    size = out_weight.shape[1] // count // PARTS

    n = len(values)

    def kernel(*refs):
        p_ref, total_ref, alpha_ref, acc_ref, w_ref, att_ref, far_ref = refs[n:]
        v = refs[0][...] if n == 1 else jnp.where(by_first_exchange(), refs[0][...], refs[1][...])
        scales = [alpha_ref[h : h + 1, :] for h in range(heads)]
        outs = value_block(v, [p_ref[h] for h in range(heads)], scales, acc_ref)
        for h, out in enumerate(outs):
            head = out * (1.0 / total_ref[h : h + 1, :])
            att_ref[:, h * HEAD_DIM : (h + 1) * HEAD_DIM] = head.T.astype(jnp.bfloat16)
        project_into(far_ref, att_ref, w_ref, None, 1, 1, 0, PARTS)

    return pl.pallas_call(
        kernel,
        out_shape=[
            jax.ShapeDtypeStruct((rows, heads * HEAD_DIM), jnp.bfloat16),
            jax.ShapeDtypeStruct((count // 4, rows, size), jnp.bfloat16),
        ],
        in_specs=[vmem] * (n + 5),
        out_specs=[vmem] * 2,
        compiler_params=params(),
        name="finish",
    )(*in_vmem([*values, weights, totals, alphas, acc]), out_weight)


def rest_call(attended, out_weight, count):
    rows, depth = attended.shape
    block = out_weight.shape[1] // count

    def kernel(att_ref, w_ref, *refs):
        for part in range(1, PARTS):
            project_into(refs[part - 1], att_ref, w_ref, None, 1, 1, part, PARTS)
        project_into(refs[-1], att_ref, w_ref, None, 1, 0, 0, 1)

    sizes = [block // PARTS] * (PARTS - 1) + [block]
    return pl.pallas_call(
        kernel,
        out_shape=[jax.ShapeDtypeStruct((count // 4, rows, size), jnp.bfloat16) for size in sizes],
        in_specs=[vmem] * 2,
        out_specs=[vmem] * PARTS,
        compiler_params=params(),
        cost_estimate=pl.CostEstimate(flops=2 * rows * depth * sum(sizes) * (count // 4), bytes_accessed=0, transcendentals=0),
        name="rest",
    )(*in_vmem([attended]), out_weight)


def project_call(attended, out_weight, added, far_core, far_next, part, parts, count, out_type, name):
    rows, depth = attended.shape
    size = out_weight.shape[1] // count // parts

    def kernel(att_ref, w_ref, *refs):
        project_into(refs[-1], att_ref, w_ref, refs[0] if len(refs) > 1 else None, far_core, far_next, part, parts)

    more = [] if added is None else [added]
    return pl.pallas_call(
        kernel,
        out_shape=jax.ShapeDtypeStruct((count // 4, rows, size), out_type),
        in_specs=[vmem] * (2 + len(more)),
        out_specs=vmem,
        compiler_params=params(),
        cost_estimate=pl.CostEstimate(flops=2 * rows * depth * size * (count // 4), bytes_accessed=0, transcendentals=0),
        name=name,
    )(*in_vmem([attended]), out_weight, *in_vmem(more))


def output_call(kept, arrived, part, whole):
    rows, size = kept.shape

    def kernel(kept_ref, arrived_ref, *refs):
        out_ref, held, sem = refs[-3:]
        held[...] = (kept_ref[...] + arrived_ref[...].astype(jnp.float32)).T.astype(jnp.bfloat16)
        copy = pltpu.make_async_copy(held, out_ref.at[part * size : (part + 1) * size], sem)
        copy.start()
        copy.wait()

    more = [] if whole is None else [in_hbm(whole)]
    return pl.pallas_call(
        kernel,
        out_shape=jax.ShapeDtypeStruct((size * PARTS, rows), jnp.bfloat16),
        in_specs=[vmem] * 2 + [hbm] * len(more),
        out_specs=hbm,
        scratch_shapes=[pltpu.VMEM((size, rows), jnp.bfloat16), pltpu.SemaphoreType.DMA],
        input_output_aliases={2: 0} if more else {},
        compiler_params=params(),
        name="output",
    )(*in_vmem([kept, arrived]), *more)


def swapped(array, axis, bit):
    return lax.ppermute(array, axis, [(i, i ^ bit) for i in range(lax.axis_size(axis))])


def summed_over_heads(attended, far, out_weight, count):
    def project(added, far_core, far_next, part, parts, out_type, name):
        return project_call(attended, out_weight, added, far_core, far_next, part, parts, count, out_type, name)

    *fars, near = rest_call(attended, out_weight, count)
    got_fars = [swapped(x, "head", 1) for x in (far, *fars)]
    sents = [project(got_fars[part], 0, 1, part, PARTS, jnp.bfloat16, "sent") for part in range(PARTS)]
    near, sents[0] = lax.optimization_barrier((near, sents[0]))
    gots = [swapped(x, "head", 2) for x in sents]
    got_near = swapped(near, "head", 1)
    kepts = [project(got_near, 0, 0, part, PARTS, jnp.float32, "kept") for part in range(PARTS)]
    me = lax.axis_index("head")
    whole = None
    for part, (kept, got) in enumerate(zip(kepts, gots)):
        for b in range(2, count.bit_length() - 1):
            kept = kept + got.astype(jnp.float32)
            pairs = kept.reshape(kept.shape[0] // 2, 2, *kept.shape[1:])
            bit = (me >> b) & 1
            sent = lax.dynamic_index_in_dim(pairs, 1 - bit, 1, keepdims=False)
            kept = lax.dynamic_index_in_dim(pairs, bit, 1, keepdims=False)
            got = swapped(sent.astype(jnp.bfloat16), "head", 1 << b)
        whole = output_call(kept[0], got[0], part, whole)
    return whole


def on_device(queries, key_vectors, value_vectors, out_weight, offsets):
    devices = lax.axis_size("ctx")
    heads = lax.axis_size("head")
    rows = queries.shape[0]
    pair_steps = (min(REACH, devices // 2) + 1) // 2

    def moved_by(array, target):
        route = []
        for position in range(devices):
            for head in range(heads):
                p, x, h = target(position // 2, position % 2, head)
                route.append((position * heads + head, (2 * p + x) * heads + h))
        return lax.ppermute(array, ("ctx", "head"), route)

    def shifted(pair, step):
        last = devices // 2 - 1

        def target(p, x, h):
            return (p, x, h ^ 1) if p < step - 1 else (p + 1 if p < last else step - 1, x, h)

        return tuple(moved_by(m, target) for m in pair)

    def across(pair, step):
        return tuple(moved_by(m, lambda p, x, h: (p, x, h ^ 1) if p < step else (p, 1 - x, h)) for m in pair)

    def exchanged(array):
        pairs = devices // 2

        def target(shift, p, x, h):
            other = ((p + shift) ^ 1) - shift
            return (other, x, h) if 0 <= other < pairs else (p, x, h ^ 1)

        return tuple(moved_by(array, lambda p, x, h, shift=shift: target(shift, p, x, h)) for shift in (0, 1))

    def after(pair, state):
        first, state = lax.optimization_barrier((pair[0], state))
        return (first, pair[1]), state

    def finished(starts, q, pair, back, state, out_weight):
        totals, alphas, weights = last_scores_call(starts, q, pair[0], back, state)
        attended, product = finish_call(pair[1:], weights, totals, alphas, state[2], out_weight, heads)
        return summed_over_heads(attended, product, out_weight, heads)

    def near(queries, key_vectors, value_vectors, out_weight, offsets):
        own = (key_vectors, value_vectors)
        moved = shifted(own, 1)
        beside = across(own, 0)
        starts, q, state = own_call(offsets, queries, key_vectors, value_vectors)
        moved, state = after(moved, state)
        crossed = across(moved[:1], 1) + exchanged(beside[1])
        state = attend_call(starts, q, *moved, lambda x: 2, state)
        state = attend_call(starts, q, *beside, lambda x: 2 * x - 1, state)
        return finished(starts, q, crossed, lambda x: 1 + 2 * x, state, out_weight)

    def reaching(queries, key_vectors, value_vectors, out_weight, offsets):
        moved = (key_vectors, value_vectors)
        beside = across(moved, 0)
        starts, q, state = own_call(offsets, queries, key_vectors, value_vectors)
        waiting = [(*beside, lambda x: 2 * x - 1)]
        for step in range(1, pair_steps + 1):
            moved = shifted(moved, step)
            if step == 1:
                moved, state = after(moved, state)
            waiting.insert(0 if step == 1 else 1, (*moved, lambda x, step=step: 2 * step))
            crossed = across(moved, step)
            if step < pair_steps:
                for piece in waiting:
                    state = attend_call(starts, q, *piece, state)
                waiting = [(*crossed, lambda x, step=step: 2 * step - 1 + 2 * x)]
        for piece in waiting:
            state = attend_call(starts, q, *piece, state)
        return finished(starts, q, crossed, lambda x: 2 * pair_steps - 1 + 2 * x, state, out_weight)

    given = (queries, key_vectors, value_vectors, out_weight, offsets)
    if pair_steps == 1:
        return near(*given)
    return lax.cond(reach_call(offsets, rows)[0] > 0, reaching, near, *given)


def solution(mesh):
    placed = (P("ctx", "head"), P("ctx", "head"), P("ctx", "head"), P("head", None), P())
    return jax.shard_map(
        on_device, mesh=mesh, in_specs=placed, out_specs=P("head", "ctx"), check_vma=False
    )
```

```python
import jax
import jax.numpy as jnp
from jax import lax
from jax.experimental import pallas as pl
from jax.experimental.pallas import tpu as pltpu
from jax.sharding import PartitionSpec as P

HEAD_DIM = 128
REACH = 15
LOG2E = 1.4426950408889634
masked_score = -1e30
PARTS = 2
VMEM_LIMIT = 20 * 1024 * 1024

vmem = pl.BlockSpec(memory_space=pltpu.VMEM)
smem = pl.BlockSpec(memory_space=pltpu.SMEM)
hbm = pl.BlockSpec(memory_space=pltpu.HBM)


def in_hbm(array):
    return pltpu.with_memory_space_constraint(array, pltpu.HBM)


def in_vmem(arrays):
    return [pltpu.with_memory_space_constraint(a, pltpu.VMEM) for a in arrays]


def params():
    return pltpu.CompilerParams(vmem_limit_bytes=VMEM_LIMIT)


def document_starts(offsets, first, rows):
    positions = first + lax.broadcasted_iota(jnp.int32, (1, rows), 1)
    starts = jnp.zeros((1, rows), jnp.int32)
    for i in range(1, offsets.shape[0] - 1):
        starts = jnp.where(positions >= offsets[i], offsets[i], starts)
    return starts


def scores_of(keys, query):
    return lax.dot_general(keys, query, (((1,), (1,)), ((), ())), preferred_element_type=jnp.float32)


def visible_keys(starts, key_start, rows, first):
    key_pos = key_start + lax.broadcasted_iota(jnp.int32, (rows, 1), 0)
    visible = key_pos >= starts
    if first is not None:
        visible = visible & (key_pos <= first + lax.broadcasted_iota(jnp.int32, (1, rows), 1))
    return visible


def score_block(q_ref, k_ref, visible, before):
    factor = HEAD_DIM ** -0.5 * LOG2E
    heads = q_ref.shape[1] // HEAD_DIM
    each = heads // (k_ref.shape[1] // HEAD_DIM)
    groups = [h // each for h in range(heads)]
    scores = [
        scores_of(k_ref[:, g * HEAD_DIM : (g + 1) * HEAD_DIM], q_ref[:, h * HEAD_DIM : (h + 1) * HEAD_DIM])
        for h, g in enumerate(groups)
    ]
    scores = [jnp.where(visible, s, masked_score) for s in scores]
    tops = [jnp.max(s, axis=0, keepdims=True) for s in scores]
    if before is not None:
        olds = [before[0][h : h + 1, :] for h in range(heads)]
        tops = [jnp.maximum(old, top) for old, top in zip(olds, tops)]
    weights = [jnp.exp2((s - top) * factor) for s, top in zip(scores, tops)]
    totals = [jnp.sum(w, axis=0, keepdims=True) for w in weights]
    weights = [w.astype(jnp.bfloat16) for w in weights]
    if before is None:
        return tops, totals, weights, None
    alphas = [jnp.exp2((old - top) * factor) for old, top in zip(olds, tops)]
    totals = [before[1][h : h + 1, :] * alphas[h] + totals[h] for h in range(heads)]
    return tops, totals, weights, alphas


def value_block(v_ref, weights, alphas, acc_ref):
    groups = v_ref.shape[1] // HEAD_DIM
    each = len(weights) // groups
    values = [v_ref[:, g * HEAD_DIM : (g + 1) * HEAD_DIM].T for g in range(groups)]
    sums = [jnp.dot(values[h // each], w, preferred_element_type=jnp.float32) for h, w in enumerate(weights)]
    if alphas is None:
        return sums
    return [acc_ref[h] * alphas[h] + s for h, s in enumerate(sums)]


def store_rows(ref, rows):
    for h, row in enumerate(rows):
        ref[h : h + 1, :] = row


def state_shapes(heads, rows):
    return [
        jax.ShapeDtypeStruct((heads, rows), jnp.float32),
        jax.ShapeDtypeStruct((heads, rows), jnp.float32),
        jax.ShapeDtypeStruct((heads, HEAD_DIM, rows), jnp.float32),
    ]


def first_row(rows):
    return lax.axis_index("ctx") * rows


def reach_call(offsets, rows):
    def kernel(offsets_ref, far_ref):
        far = jnp.int32(0)
        for i in range(offsets_ref.shape[0] - 1):
            steps = (offsets_ref[i + 1] - 1) // (2 * rows) - offsets_ref[i] // (2 * rows)
            far = jnp.maximum(far, jnp.where(steps >= 2, 1, 0))
        far_ref[0] = far

    return pl.pallas_call(
        kernel,
        out_shape=pltpu.SMEM((1,), jnp.int32),
        in_specs=[smem],
        out_specs=smem,
        name="reach",
    )(in_hbm(offsets))


def own_call(offsets, q, keys, values):
    rows, width = q.shape

    def kernel(offsets_in, q_in, k_in, v_in, starts_ref, q_ref, top_ref, total_ref, acc_ref, offsets_ref, k_ref, v_ref, sems):
        copies = [
            pltpu.make_async_copy(source, target, sems.at[i])
            for i, (source, target) in enumerate(((offsets_in, offsets_ref), (k_in, k_ref), (q_in, q_ref), (v_in, v_ref)))
        ]
        for copy in copies:
            copy.start()
        copies[0].wait()
        first = first_row(rows)
        starts = document_starts(offsets_ref, first, rows)
        starts_ref[...] = starts
        visible = visible_keys(starts, first, rows, first)
        for copy in copies[1:3]:
            copy.wait()
        tops, totals, weights, _ = score_block(q_ref, k_ref, visible, None)
        copies[3].wait()
        store_rows(top_ref, tops)
        store_rows(total_ref, totals)
        for h, out in enumerate(value_block(v_ref, weights, None, None)):
            acc_ref[h] = out

    outs = pl.pallas_call(
        kernel,
        out_shape=[
            jax.ShapeDtypeStruct((1, rows), jnp.int32),
            jax.ShapeDtypeStruct(q.shape, q.dtype),
            *state_shapes(width // HEAD_DIM, rows),
        ],
        in_specs=[hbm] * 4,
        out_specs=[vmem] * 5,
        scratch_shapes=[
            pltpu.SMEM(offsets.shape, offsets.dtype),
            *[pltpu.VMEM(x.shape, x.dtype) for x in (keys, values)],
            pltpu.SemaphoreType.DMA((4,)),
        ],
        compiler_params=params(),
        cost_estimate=cost(width, rows, 1),
        name="own",
    )(*[in_hbm(x) for x in (offsets, q, keys, values)])
    return *outs[:2], outs[2:]


def cost(width, rows, blocks):
    return pl.CostEstimate(flops=20 * width * rows * rows * blocks, bytes_accessed=0, transcendentals=0)


def reached(back, rows):
    position = lax.axis_index("ctx")
    block = position - back(lax.rem(position, 2))
    return block * rows, (block >= 0) & (block <= position)


def attend_call(starts, q, keys, values, back, state):
    rows, width = q.shape

    def kernel(starts_ref, q_ref, k_ref, v_ref, *refs):
        before, after = refs[:3], refs[3:]
        key_start, seen = reached(back, rows)

        @pl.when(seen)
        def _():
            visible = visible_keys(starts_ref[...], key_start, rows, None)
            tops, totals, weights, alphas = score_block(q_ref, k_ref, visible, before)
            store_rows(after[0], tops)
            store_rows(after[1], totals)
            for h, out in enumerate(value_block(v_ref, weights, alphas, before[2])):
                after[2][h] = out

        @pl.when(jnp.logical_not(seen))
        def _():
            for old, new in zip(before, after):
                new[...] = old[...]

    return pl.pallas_call(
        kernel,
        out_shape=state_shapes(width // HEAD_DIM, rows),
        in_specs=[vmem] * 7,
        out_specs=[vmem] * 3,
        input_output_aliases={4 + i: i for i in range(3)},
        compiler_params=params(),
        cost_estimate=cost(width, rows, 1),
        name="attend",
    )(*in_vmem([starts, q, keys, values, *state]))


def last_scores_call(starts, q, keys, back, state):
    rows, width = q.shape
    heads = width // HEAD_DIM

    def kernel(starts_ref, q_ref, k_ref, top_ref, old_total_ref, total_ref, alpha_ref, weights_ref):
        key_start, seen = reached(back, rows)

        @pl.when(seen)
        def _():
            visible = visible_keys(starts_ref[...], key_start, rows, None)
            _, totals, weights, alphas = score_block(q_ref, k_ref, visible, (top_ref, old_total_ref))
            store_rows(total_ref, totals)
            store_rows(alpha_ref, alphas)
            for h, w in enumerate(weights):
                weights_ref[h] = w

        @pl.when(jnp.logical_not(seen))
        def _():
            total_ref[...] = old_total_ref[...]
            alpha_ref[...] = jnp.ones_like(alpha_ref)
            weights_ref[...] = jnp.zeros_like(weights_ref)

    return pl.pallas_call(
        kernel,
        out_shape=[
            jax.ShapeDtypeStruct((heads, rows), jnp.float32),
            jax.ShapeDtypeStruct((heads, rows), jnp.float32),
            jax.ShapeDtypeStruct((heads, rows, rows), jnp.bfloat16),
        ],
        in_specs=[vmem] * 5,
        out_specs=[vmem] * 3,
        compiler_params=params(),
        cost_estimate=cost(width, rows, 1),
        name="last_scores",
    )(*in_vmem([starts, q, keys, state[0], state[1]]))


def project_into(out_ref, att_ref, w_ref, added_ref, far_core, far_next, part, parts):
    size = out_ref.shape[2]
    block = size * parts
    added_start = 0 if added_ref is None or added_ref.shape[2] == size else part * size
    step = min(size, 256)
    me = lax.axis_index("head")
    bits = (me % 2 + far_core) % 2 + 2 * ((me // 2 + far_next) % 2)
    first = pl.multiple_of(bits * block, block)
    for i in range(out_ref.shape[0]):
        for start in range(0, size, step):
            cut = slice(start, start + step)
            columns = w_ref[:, pl.ds(first + 4 * i * block + part * size + start, step)]
            value = jnp.dot(att_ref[...], columns, preferred_element_type=jnp.float32)
            if added_ref is not None:
                value = value + added_ref[i, :, added_start + start : added_start + start + step].astype(jnp.float32)
            out_ref[i, :, cut] = value.astype(out_ref.dtype)


def by_first_exchange():
    return lax.rem(lax.axis_index("ctx") // 2, 2) == 1


def finish_call(values, weights, totals, alphas, acc, out_weight, count):
    heads, _, rows = acc.shape
    size = out_weight.shape[1] // count // PARTS

    n = len(values)

    def kernel(*refs):
        p_ref, total_ref, alpha_ref, acc_ref, w_ref, att_ref, far_ref = refs[n:]
        v = refs[0][...] if n == 1 else jnp.where(by_first_exchange(), refs[0][...], refs[1][...])
        scales = [alpha_ref[h : h + 1, :] for h in range(heads)]
        outs = value_block(v, [p_ref[h] for h in range(heads)], scales, acc_ref)
        for h, out in enumerate(outs):
            head = out * (1.0 / total_ref[h : h + 1, :])
            att_ref[:, h * HEAD_DIM : (h + 1) * HEAD_DIM] = head.T.astype(jnp.bfloat16)
        project_into(far_ref, att_ref, w_ref, None, 1, 1, 0, PARTS)

    return pl.pallas_call(
        kernel,
        out_shape=[
            jax.ShapeDtypeStruct((rows, heads * HEAD_DIM), jnp.bfloat16),
            jax.ShapeDtypeStruct((count // 4, rows, size), jnp.bfloat16),
        ],
        in_specs=[vmem] * (n + 5),
        out_specs=[vmem] * 2,
        compiler_params=params(),
        name="finish",
    )(*in_vmem([*values, weights, totals, alphas, acc]), out_weight)


def rest_call(attended, out_weight, count):
    rows, depth = attended.shape
    block = out_weight.shape[1] // count

    def kernel(att_ref, w_ref, *refs):
        for part in range(1, PARTS):
            project_into(refs[part - 1], att_ref, w_ref, None, 1, 1, part, PARTS)
        project_into(refs[-1], att_ref, w_ref, None, 1, 0, 0, 1)

    sizes = [block // PARTS] * (PARTS - 1) + [block]
    return pl.pallas_call(
        kernel,
        out_shape=[jax.ShapeDtypeStruct((count // 4, rows, size), jnp.bfloat16) for size in sizes],
        in_specs=[vmem] * 2,
        out_specs=[vmem] * PARTS,
        compiler_params=params(),
        cost_estimate=pl.CostEstimate(flops=2 * rows * depth * sum(sizes) * (count // 4), bytes_accessed=0, transcendentals=0),
        name="rest",
    )(*in_vmem([attended]), out_weight)


def project_call(attended, out_weight, added, far_core, far_next, part, parts, count, out_type, name):
    rows, depth = attended.shape
    size = out_weight.shape[1] // count // parts

    def kernel(att_ref, w_ref, *refs):
        project_into(refs[-1], att_ref, w_ref, refs[0] if len(refs) > 1 else None, far_core, far_next, part, parts)

    more = [] if added is None else [added]
    return pl.pallas_call(
        kernel,
        out_shape=jax.ShapeDtypeStruct((count // 4, rows, size), out_type),
        in_specs=[vmem] * (2 + len(more)),
        out_specs=vmem,
        compiler_params=params(),
        cost_estimate=pl.CostEstimate(flops=2 * rows * depth * size * (count // 4), bytes_accessed=0, transcendentals=0),
        name=name,
    )(*in_vmem([attended]), out_weight, *in_vmem(more))


def output_call(kept, arrived, part, whole):
    rows, size = kept.shape

    def kernel(kept_ref, arrived_ref, *refs):
        out_ref, held, sem = refs[-3:]
        held[...] = (kept_ref[...] + arrived_ref[...].astype(jnp.float32)).T.astype(jnp.bfloat16)
        copy = pltpu.make_async_copy(held, out_ref.at[part * size : (part + 1) * size], sem)
        copy.start()
        copy.wait()

    more = [] if whole is None else [in_hbm(whole)]
    return pl.pallas_call(
        kernel,
        out_shape=jax.ShapeDtypeStruct((size * PARTS, rows), jnp.bfloat16),
        in_specs=[vmem] * 2 + [hbm] * len(more),
        out_specs=hbm,
        scratch_shapes=[pltpu.VMEM((size, rows), jnp.bfloat16), pltpu.SemaphoreType.DMA],
        input_output_aliases={2: 0} if more else {},
        compiler_params=params(),
        name="output",
    )(*in_vmem([kept, arrived]), *more)


def swapped(array, axis, bit):
    return lax.ppermute(array, axis, [(i, i ^ bit) for i in range(lax.axis_size(axis))])


def summed_over_heads(attended, far, out_weight, count):
    def project(added, far_core, far_next, part, parts, out_type, name):
        return project_call(attended, out_weight, added, far_core, far_next, part, parts, count, out_type, name)

    *fars, near = rest_call(attended, out_weight, count)
    got_fars = [swapped(x, "head", 1) for x in (far, *fars)]
    sents = [project(got_fars[part], 0, 1, part, PARTS, jnp.bfloat16, "sent") for part in range(PARTS)]
    near, sents[0] = lax.optimization_barrier((near, sents[0]))
    gots = [swapped(x, "head", 2) for x in sents]
    got_near = swapped(near, "head", 1)
    kepts = [project(got_near, 0, 0, part, PARTS, jnp.float32, "kept") for part in range(PARTS)]
    me = lax.axis_index("head")
    whole = None
    for part, (kept, got) in enumerate(zip(kepts, gots)):
        for b in range(2, count.bit_length() - 1):
            kept = kept + got.astype(jnp.float32)
            pairs = kept.reshape(kept.shape[0] // 2, 2, *kept.shape[1:])
            bit = (me >> b) & 1
            sent = lax.dynamic_index_in_dim(pairs, 1 - bit, 1, keepdims=False)
            kept = lax.dynamic_index_in_dim(pairs, bit, 1, keepdims=False)
            got = swapped(sent.astype(jnp.bfloat16), "head", 1 << b)
        whole = output_call(kept[0], got[0], part, whole)
    return whole


def on_device(queries, key_vectors, value_vectors, out_weight, offsets):
    devices = lax.axis_size("ctx")
    heads = lax.axis_size("head")
    rows = queries.shape[0]
    pair_steps = (min(REACH, devices // 2) + 1) // 2

    def moved_by(array, target):
        route = []
        for position in range(devices):
            for head in range(heads):
                p, x, h = target(position // 2, position % 2, head)
                route.append((position * heads + head, (2 * p + x) * heads + h))
        return lax.ppermute(array, ("ctx", "head"), route)

    def shifted(pair, step):
        last = devices // 2 - 1

        def target(p, x, h):
            return (p, x, h ^ 1) if p < step - 1 else (p + 1 if p < last else step - 1, x, h)

        return tuple(moved_by(m, target) for m in pair)

    def across(pair, step):
        return tuple(moved_by(m, lambda p, x, h: (p, x, h ^ 1) if p < step else (p, 1 - x, h)) for m in pair)

    def exchanged(array):
        pairs = devices // 2

        def target(shift, p, x, h):
            other = ((p + shift) ^ 1) - shift
            return (other, x, h) if 0 <= other < pairs else (p, x, h ^ 1)

        return tuple(moved_by(array, lambda p, x, h, shift=shift: target(shift, p, x, h)) for shift in (0, 1))

    def after(pair, state):
        first, state = lax.optimization_barrier((pair[0], state))
        return (first, pair[1]), state

    def finished(starts, q, pair, back, state, out_weight):
        totals, alphas, weights = last_scores_call(starts, q, pair[0], back, state)
        attended, product = finish_call(pair[1:], weights, totals, alphas, state[2], out_weight, heads)
        return summed_over_heads(attended, product, out_weight, heads)

    def near(queries, key_vectors, value_vectors, out_weight, offsets):
        own = (key_vectors, value_vectors)
        moved = shifted(own, 1)
        beside = across(own, 0)
        starts, q, state = own_call(offsets, queries, key_vectors, value_vectors)
        moved, state = after(moved, state)
        crossed = across(moved[:1], 1) + exchanged(beside[1])
        state = attend_call(starts, q, *moved, lambda x: 2, state)
        state = attend_call(starts, q, *beside, lambda x: 2 * x - 1, state)
        return finished(starts, q, crossed, lambda x: 1 + 2 * x, state, out_weight)

    def reaching(queries, key_vectors, value_vectors, out_weight, offsets):
        moved = (key_vectors, value_vectors)
        beside = across(moved, 0)
        starts, q, state = own_call(offsets, queries, key_vectors, value_vectors)
        waiting = [(*beside, lambda x: 2 * x - 1)]
        for step in range(1, pair_steps + 1):
            moved = shifted(moved, step)
            if step == 1:
                moved, state = after(moved, state)
            waiting.insert(0 if step == 1 else 1, (*moved, lambda x, step=step: 2 * step))
            crossed = across(moved, step)
            if step < pair_steps:
                for piece in waiting:
                    state = attend_call(starts, q, *piece, state)
                waiting = [(*crossed, lambda x, step=step: 2 * step - 1 + 2 * x)]
        for piece in waiting:
            state = attend_call(starts, q, *piece, state)
        return finished(starts, q, crossed, lambda x: 2 * pair_steps - 1 + 2 * x, state, out_weight)

    given = (queries, key_vectors, value_vectors, out_weight, offsets)
    if pair_steps == 1:
        return near(*given)
    return lax.cond(reach_call(offsets, rows)[0] > 0, reaching, near, *given)


def solution(mesh):
    placed = (P("ctx", "head"), P("ctx", "head"), P("ctx", "head"), P("head", None), P())
    return jax.shard_map(
        on_device, mesh=mesh, in_specs=placed, out_specs=P("head", "ctx"), check_vma=False
    )
```
